256 devices in a mesh: beam: 4 (over z_lo, core), det: 16 (over y, x), slab: 4 (over z_hi).
Axes of the slice: x: 4, y: 4, z: 8 (z_hi: 4, z_lo: 2; z = z_hi * 2 + z_lo), core: 2. Of those that a mesh axis runs over, the one named last changes fastest.
Arguments:
- concentration: float32 [4, 32, 1024, 2048], P(None, 'slab', 'beam', 'det'), may hold values from 0.1 to 1
- cross_section: float32 [4, 16], replicated, may hold values from 0.2 to 2
- line_attenuation: float32 [4], replicated, may hold values from 0.5 to 2
- energy_index: int32 [4], replicated, may hold values from 0 to 15
- fan_offset: int32 [256], replicated, may hold values from 0 to 28
- fan_weight: int32 [256, 4], replicated, may hold values from 1 to 3
- measured: float32 [4, 256, 2048], P(None, None, 'det'), may hold values from 0 to 6
Outputs:
- voxel_grad: float32 [4, 32, 1024, 2048], P(None, 'slab', 'beam', 'det')
- residual: float32 [4, 256, 2048], P(None, ('beam', 'slab'), 'det')
The draws below stay inside these ranges and needn't reach their ends.
All inputs are finite; a program needn't handle non-finite values.
Results may differ from the reference program's by a relative error of at most 0.00013.
Values sent between devices are 32-bit elements; how exact they have to be, the bound alone decides.
A program may use at most 128 MiB of HBM per device.

```python
import math
import jax
import jax.numpy as jnp
from jax import lax

S = 4
ENERGIES = 16
E_WIN = 4
K = 256
FAN = 4
NX = 1024
NY = 2048
NZ = 32


def place_ends(drawn, own_key, smallest, largest):
    spot = [jax.random.randint(jax.random.fold_in(own_key, axis), (), 0, length) for axis, length in enumerate(drawn.shape)]
    main_axis = drawn.shape.index(max(drawn.shape))
    neighbour = spot[:main_axis] + [(spot[main_axis] + 1) % drawn.shape[main_axis]] + spot[main_axis + 1:]
    return drawn.at[tuple(spot)].set(smallest).at[tuple(neighbour)].set(largest)


def level_of(stream_key, shape, cuts, low, high):
    level, own = 1.0, jax.random.fold_in(stream_key, 6)
    for position, parts in cuts:
        draws = jnp.exp(jax.random.uniform(jax.random.fold_in(own, position), (parts,), jnp.float32, low / len(cuts), high / len(cuts)))
        level = level * jnp.repeat(draws, shape[position] // parts).reshape([-1 if axis == position else 1 for axis in range(len(shape))])
    return level


def setup_inputs(seed: int = 0) -> dict:
    seeds = jax.random.split(jax.random.key(seed), 8)
    return {
        "concentration": jnp.clip(jnp.exp(math.log(1.0) - 2.3025851 * jax.random.uniform(seeds[0], (S, NZ, NX, NY), jnp.float32) ** level_of(seeds[0], (S, NZ, NX, NY), ((1, 4), (2, 4), (3, 16)), -0.2, 0.2)), 0.1, 1.0),
        "cross_section": jnp.clip(jnp.exp(jax.random.uniform(seeds[1], (S, ENERGIES), jnp.float32, math.log(0.2), math.log(2.0))), 0.2, 2.0),
        "line_attenuation": jnp.clip(jnp.exp(jax.random.uniform(seeds[2], (S,), jnp.float32, math.log(0.5), math.log(2.0))), 0.5, 2.0),
        "energy_index": place_ends(jax.random.randint(seeds[3], (E_WIN,), 0, ENERGIES), jax.random.fold_in(seeds[3], 1), 0, ENERGIES - 1).astype(jnp.int32),
        "fan_offset": place_ends(jax.random.randint(seeds[4], (K,), 0, NZ - FAN + 1), jax.random.fold_in(seeds[4], 1), 0, NZ - FAN).astype(jnp.int32),
        "fan_weight": place_ends(jax.random.randint(seeds[5], (K, FAN), 1, 4), jax.random.fold_in(seeds[5], 1), 1, 3).astype(jnp.int32),
        "measured": jnp.clip(6.0 * jax.random.uniform(seeds[6], (E_WIN, K, NY), jnp.float32) ** level_of(seeds[6], (E_WIN, K, NY), ((2, 16),), -0.2, 0.2), 0.0, 6.0),
    }


def fan_matrix(fan_offset, fan_weight, slices):
    taps = fan_offset[:, None] + jnp.arange(fan_weight.shape[1], dtype=jnp.int32)[None, :]
    match = (taps[:, :, None] == slices[None, None, :]).astype(jnp.float32)
    return jnp.sum(fan_weight.astype(jnp.float32)[:, :, None] * match, axis=1)


def attenuate(conc_slice, sigma_sel, line_attenuation):
    emission = sigma_sel[0][:, None, None] * conc_slice[0][None]
    absorber = line_attenuation[0] * conc_slice[0]
    for species in range(1, S):
        emission = emission + sigma_sel[species][:, None, None] * conc_slice[species][None]
        absorber = absorber + line_attenuation[species] * conc_slice[species]
    path_in = jnp.cumsum(emission, axis=1) - emission
    incident = jnp.exp(-(1.5 / NX) * path_in)
    path_out = jnp.sum(absorber, axis=1, keepdims=True) - jnp.cumsum(absorber, axis=1)
    escape = jnp.exp(-(1.5 / NY) * path_out)
    return emission, incident, escape


def reference(concentration, cross_section, line_attenuation, energy_index, fan_offset, fan_weight, measured):
    hi = lax.Precision.HIGHEST
    sigma_sel = cross_section[:, energy_index]
    weights = fan_matrix(fan_offset, fan_weight, jnp.arange(NZ, dtype=jnp.int32))

    def forward(slice_index):
        conc_slice = concentration[:, slice_index]
        emission, incident, escape = attenuate(conc_slice, sigma_sel, line_attenuation)
        return jnp.sum(emission * incident * escape[None], axis=1)

    line_sums = lax.map(forward, jnp.arange(NZ, dtype=jnp.int32))
    signal = jnp.einsum("kz,zey->eky", weights, line_sums, precision=hi) / NX
    residual = signal - measured
    back = jnp.einsum("kz,eky->zey", weights, residual, precision=hi)

    def backward(slice_index):
        conc_slice = concentration[:, slice_index]
        emission, incident, escape = attenuate(conc_slice, sigma_sel, line_attenuation)
        fluor = emission * incident * escape[None]
        back_z = back[slice_index]
        heavy = back_z[:, None, :] * fluor
        after_x = jnp.sum(heavy, axis=1, keepdims=True) - jnp.cumsum(heavy, axis=1)
        summed = jnp.sum(heavy, axis=0)
        before_y = jnp.cumsum(summed, axis=1) - summed
        term = back_z[:, None, :] * incident * escape[None] - (1.5 / NX) * after_x
        result = []
        for species in range(S):
            acc = sigma_sel[species, 0] * term[0]
            for energy in range(1, E_WIN):
                acc = acc + sigma_sel[species, energy] * term[energy]
            result.append(acc - line_attenuation[species] * (1.5 / NY) * before_y)
        return jnp.stack(result)

    grads = lax.map(backward, jnp.arange(NZ, dtype=jnp.int32))
    return jnp.moveaxis(grads, 0, 1), residual
```

```python
import functools

import jax
import jax.numpy as jnp
from jax import lax
from jax.experimental import pallas as pl
from jax.experimental.pallas import tpu as pltpu
from jax.sharding import PartitionSpec as P

MESH = pl.DeviceIdType.MESH
F32 = jnp.float32
BF16 = jnp.bfloat16
HIGHEST = lax.Precision.HIGHEST
CHUNKS = 4
BLOCK = 16
REACH = 3


def split_pair(value):
    high = value.astype(BF16)
    low = (value - high.astype(F32)).astype(BF16)
    return jnp.concatenate([high, low], axis=1)


def row_totals(pair):
    ones = jnp.ones((8, pair.shape[1]), BF16)
    total = lax.dot_general(ones, pair, (((1,), (1,)), ((), ())), preferred_element_type=F32)
    return total[0:1]


def spread(compact):
    rows = compact.shape[0]
    padded = jnp.concatenate([compact, jnp.zeros((128 - rows, 128), F32)], axis=0)
    turned = jnp.transpose(padded)
    return [jnp.broadcast_to(turned[:, r : r + 1], (128, 128)) for r in range(rows)]


def kernel(
    sizes, conc, cross, lam, index, offset, weight, measured, out, resid,
    c_buf, em, inc, dmp, hl, meas, wt, wx, wk, band, wm, up_buf,
    ra_send, ra_recv, ud_send, ud_recv, x_buf, xl, la, rc_send, rc_recv,
    in_sem, meas_sem, ra_ss, ra_rs, ud_ss, ud_rs, x_ss, x_rs, la_ss, la_rs, rc_ss, rc_rs, out_sem,
):
    n_beam, n_det, n_slab = sizes
    n_s, nz, nx, ny = conc.shape
    n_e = measured.shape[0]
    n_k = measured.shape[1]
    fan = weight.shape[0]
    c1 = 1.5 / (nx * n_beam)
    c2 = 1.5 / (ny * n_det)
    blocks = nx // BLOCK
    step = nx // CHUNKS
    per_chunk = blocks // CHUNKS
    beam, det, slab = lax.axis_index("beam"), lax.axis_index("det"), lax.axis_index("slab")

    def load(chunk, z):
        rows = pl.ds(chunk * step, step)
        return pltpu.make_async_copy(conc.at[:, z, rows, :], c_buf.at[:, rows, z, :], in_sem.at[chunk, z])

    for chunk in range(CHUNKS):
        for z in range(nz):
            load(chunk, z).start()
    load_measured = pltpu.make_async_copy(measured, meas, meas_sem)
    load_measured.start()

    def beam_at(away):
        return lax.rem(beam + away, n_beam)

    def slab_at(away):
        return lax.rem(slab + away, n_slab)

    halo = (1, n_slab - 1)
    peers = [{"det": lax.rem(det + away, n_det)} for away in range(1, n_det)]
    for slab_away in range(n_slab):
        for beam_away in range(n_beam):
            if slab_away == 0 and beam_away == 0:
                continue
            if slab_away == 0 or slab_away in halo or beam_away == 0:
                peers.append({"beam": beam_at(beam_away), "slab": slab_at(slab_away)})
    barrier = pltpu.get_barrier_semaphore()
    for peer in peers:
        pl.semaphore_signal(barrier, inc=1, device_id=peer, device_id_type=MESH)

    def remote(src, dst, send, recv, device):
        return pltpu.make_async_remote_copy(
            src_ref=src, dst_ref=dst, send_sem=send, recv_sem=recv, device_id=device, device_id_type=MESH
        )

    def depth_copy(away):
        return remote(ra_send, ra_recv.at[away], ra_ss.at[away], ra_rs.at[away], {"det": lax.rem(det - away + n_det, n_det)})

    def column_copy(away):
        return remote(rc_send, rc_recv.at[away], rc_ss.at[away], rc_rs.at[away], {"det": lax.rem(det + away, n_det)})

    def beam_copy(away):
        slot = n_beam - away
        return remote(ud_send, ud_recv.at[slot], ud_ss.at[away], ud_rs.at[slot], {"beam": beam_at(away)})

    def line_copy(part, away):
        slot = (n_beam - away) % n_beam
        if part == 1:
            src, rows, target = x_buf.at[0, :, pl.ds(nz, nz), :], pl.ds(nz, nz), slab
        elif part == 0:
            src, rows, target = x_buf.at[0, :, pl.ds(2 * nz - REACH, REACH), :], pl.ds(nz - REACH, REACH), slab_at(1)
        else:
            src, rows, target = x_buf.at[0, :, pl.ds(nz, REACH), :], pl.ds(2 * nz, REACH), slab_at(n_slab - 1)
        return remote(
            src, x_buf.at[slot, :, rows, :], x_ss.at[part, away], x_rs.at[part, slot], {"beam": beam_at(away), "slab": target}
        )

    def slab_copy(away, receiving):
        source = slab_at(away) if receiving else slab
        rows = pl.ds(pl.multiple_of(source * nz, nz), nz)
        slot = away if receiving else n_slab - away
        return remote(
            xl.at[:, pl.ds(nz, nz), :], la.at[:, rows, :], la_ss.at[away], la_rs.at[slot], {"slab": slab_at(away)}
        )

    sigma = [[cross[s, index[e]] * c1 for e in range(n_e)] for s in range(n_s)]
    lam_near = [lam[s] * c2 for s in range(n_s)]
    lam_before = [lam[s] * (c2 / c1) for s in range(n_s)]

    def first(block, depth):
        depth = list(depth)
        absorb = []
        for part in range(BLOCK // 4):
            rows = pl.ds(block * BLOCK + part * 4, 4)
            c = [c_buf[s, rows] for s in range(n_s)]
            ab = lam_near[0] * c[0]
            for s in range(1, n_s):
                ab = ab + lam_near[s] * c[s]
            absorb.append(ab)
            for e in range(n_e):
                value = sigma[0][e] * c[0]
                for s in range(1, n_s):
                    value = value + sigma[s][e] * c[s]
                em[e, rows] = value
                for x in range(4):
                    inc[e, block * BLOCK + part * 4 + x] = jnp.exp(-depth[e])
                    depth[e] = depth[e] + value[x]
        pair = split_pair(jnp.concatenate(absorb, axis=0).reshape(BLOCK * nz, ny))
        hl[block] = pair
        ra_send[pl.ds(block, 1), :] = row_totals(pair)
        return tuple(depth)

    depth = (jnp.zeros((nz, ny), F32),) * n_e
    for chunk in range(CHUNKS):
        for z in range(nz):
            load(chunk, z).wait()
        depth = lax.fori_loop(chunk * per_chunk, (chunk + 1) * per_chunk, first, depth)
    for e in range(n_e):
        ud_send[e] = depth[e]

    pl.semaphore_wait(barrier, len(peers))
    for away in range(1, n_det):

        @pl.when(det - away >= 0)
        def _():
            depth_copy(away).start()

    for away in range(1, n_beam):
        beam_copy(away).start()

    for away in range(1, n_det):

        @pl.when(det + away >= n_det)
        def _():
            ra_recv[away] = jnp.zeros_like(ra_send)

        @pl.when(det - away < 0)
        def _():
            rc_recv[away] = jnp.zeros_like(rc_send)

    deep = lax.broadcasted_iota(jnp.int32, (2 * ny, ny), 0) % ny
    wide = lax.broadcasted_iota(jnp.int32, (2 * ny, ny), 1)
    beyond = jnp.where(deep > wide, 1.0, 0.0).astype(BF16)
    nearer_side = jnp.where(deep < wide, 1.0, 0.0).astype(BF16)

    def second(block, carry):
        path = jnp.dot(hl[block], beyond, preferred_element_type=F32)
        escape = jnp.exp(-path).reshape(BLOCK, nz, ny)
        rows = pl.ds(block * BLOCK, BLOCK)
        for e in range(n_e):
            light = inc[e, rows] * escape
            inc[e, rows] = light
            em[e, rows] = em[e, rows] * light
        return carry

    lax.fori_loop(0, blocks, second, 0)

    slices = lax.broadcasted_iota(jnp.int32, wt.shape, 0) - nz
    full = jnp.zeros(wt.shape, F32)
    for j in range(fan):
        tap = weight[j : j + 1, :].astype(F32)
        full = full + jnp.where(offset[...] + j == slices, tap, 0.0)
    wt[...] = full
    wx[...] = wt[pl.ds(pl.multiple_of(slab * nz, nz), 3 * nz), :]
    whole = wt[nz : nz + n_slab * nz, :]
    padded = jnp.concatenate([whole, jnp.zeros((128 - n_slab * nz, n_k), F32)], axis=0)
    wk[...] = jnp.transpose(padded)
    own = wx[nz : 2 * nz, :]
    for shift in range(2 * REACH + 1):
        other = wx[nz - REACH + shift : 2 * nz - REACH + shift, :]
        band[shift] = jnp.broadcast_to(jnp.sum(own * other, axis=1, keepdims=True), (nz, ny))
    load_measured.wait()
    for e in range(n_e):
        wm[e] = jnp.dot(own, meas[e], precision=HIGHEST, preferred_element_type=F32)

    for away in range(1, n_beam):
        beam_copy(away).wait_recv()
    upstream = jnp.zeros((n_e, nz, ny), F32)
    for slot in range(1, n_beam):
        upstream = upstream + jnp.where(beam + slot >= n_beam, 1.0, 0.0) * ud_recv[slot]
    up_buf[...] = jnp.exp(-upstream)

    for away in range(1, n_det):

        @pl.when(det + away < n_det)
        def _():
            depth_copy(away).wait_recv()

    downstream = ra_recv[1]
    for away in range(2, n_det):
        downstream = downstream + ra_recv[away]
    for r, piece in enumerate(spread(jnp.exp(-downstream))):
        dmp[r * BLOCK : (r + 1) * BLOCK] = piece.reshape(BLOCK, nz, ny)

    def third(block, sums):
        rows = pl.ds(block * BLOCK, BLOCK)
        damp = dmp[rows]
        return tuple(sums[e] + jnp.sum(em[e, rows] * damp, axis=0) for e in range(n_e))

    sums = lax.fori_loop(0, blocks, third, (jnp.zeros((nz, ny), F32),) * n_e)
    for e in range(n_e):
        x_buf[0, e, nz : 2 * nz] = sums[e] * up_buf[e]
    for away in range(n_beam):
        for part in (1, 0, 2):
            if part == 1 and away == 0:
                continue
            line_copy(part, away).start()

    def fourth(count, after):
        block = blocks - 1 - count
        after = list(after)
        for x in range(BLOCK - 1, -1, -1):
            row = block * BLOCK + x
            damp = dmp[row]
            for e in range(n_e):
                fluor = em[e, row] * damp
                inc[e, row] = inc[e, row] * damp - after[e]
                em[e, row] = fluor
                after[e] = after[e] + fluor
        return tuple(after)

    lax.fori_loop(0, blocks, fourth, (jnp.zeros((nz, ny), F32),) * n_e)

    for away in range(n_beam):
        for part in (1, 0, 2):
            if part == 1 and away == 0:
                continue
            line_copy(part, away).wait_recv()
    near = slice(nz - REACH, 2 * nz + REACH)
    extent = x_buf[0, :, near]
    for slot in range(1, n_beam):
        extent = extent + x_buf[slot, :, near]
    xl[:, near] = extent
    further = jnp.zeros((n_e, nz, ny), F32)
    for slot in range(1, n_beam):
        further = further + jnp.where(beam + slot < n_beam, 1.0, 0.0) * x_buf[slot, :, nz : 2 * nz]
    back = []
    for e in range(n_e):
        value = band[0] * xl[e, nz - REACH : 2 * nz - REACH]
        for shift in range(1, 2 * REACH + 1):
            value = value + band[shift] * xl[e, nz - REACH + shift : 2 * nz - REACH + shift]
        back.append(value * (1.0 / 1.5) - wm[e])
    lit = [back[e] * up_buf[e] for e in range(n_e)]

    def fifth(block, carry):
        rows = pl.ds(block * BLOCK, BLOCK)
        heavy = lit[0] * em[0, rows]
        for e in range(1, n_e):
            heavy = heavy + lit[e] * em[e, rows]
        pair = split_pair(heavy.reshape(BLOCK * nz, ny))
        hl[block] = pair
        rc_send[pl.ds(block, 1), :] = row_totals(pair)
        return carry

    lax.fori_loop(0, blocks, fifth, 0)
    for away in range(1, n_det):

        @pl.when(det + away < n_det)
        def _():
            column_copy(away).start()

    for away in range(1, n_slab):
        slab_copy(away, False).start()
    la[:, pl.ds(pl.multiple_of(slab * nz, nz), nz), :] = xl[:, nz : 2 * nz, :]
    shade = [back[e] * further[e] for e in range(n_e)]
    mix, less = [], []
    for s in range(n_s):
        pull = [cross[s, index[e]] for e in range(n_e)]
        mix.append([pull[e] * lit[e] for e in range(n_e)])
        value = pull[0] * shade[0]
        for e in range(1, n_e):
            value = value + pull[e] * shade[e]
        less.append(value)

    def sixth(block, carry):
        before = jnp.dot(hl[block], nearer_side, preferred_element_type=F32).reshape(BLOCK, nz, ny)
        for part in range(BLOCK // 4):
            rows = pl.ds(block * BLOCK + part * 4, 4)
            term = [inc[e, rows] for e in range(n_e)]
            for s in range(n_s):
                value = mix[s][0] * term[0]
                for e in range(1, n_e):
                    value = value + mix[s][e] * term[e]
                c_buf[s, rows] = value - less[s] - lam_before[s] * before[part * 4 : part * 4 + 4]
        return carry

    lax.fori_loop(0, blocks, sixth, 0)

    for away in range(1, n_slab):
        slab_copy(away, True).wait_recv()
    share = n_k // (n_beam * n_slab)
    mine = pl.ds(pl.multiple_of((beam * n_slab + slab) * share, share), share)
    for e in range(n_e):
        signal = jnp.dot(wk[mine, 0 : n_slab * nz], la[e], precision=HIGHEST, preferred_element_type=F32)
        resid[e] = signal * (1.0 / 1.5) - meas[e, mine]

    for away in range(1, n_det):

        @pl.when(det - away >= 0)
        def _():
            remote(rc_send, rc_recv.at[away], rc_ss.at[away], rc_rs.at[away], {"det": lax.rem(det + away, n_det)}).wait_recv()

    nearer = rc_recv[1]
    for away in range(2, n_det):
        nearer = nearer + rc_recv[away]
    for r, piece in enumerate(spread(nearer)):
        dmp[r * BLOCK : (r + 1) * BLOCK] = piece.reshape(BLOCK, nz, ny)

    def store(chunk, z):
        rows = pl.ds(chunk * step, step)
        return pltpu.make_async_copy(c_buf.at[:, rows, z, :], out.at[:, z, rows, :], out_sem.at[chunk, z])

    def seventh(block, carry):
        rows = pl.ds(block * BLOCK, BLOCK)
        shift = dmp[rows]
        for s in range(n_s):
            c_buf[s, rows] = c_buf[s, rows] - lam_before[s] * shift
        return carry

    for chunk in range(CHUNKS):
        lax.fori_loop(chunk * per_chunk, (chunk + 1) * per_chunk, seventh, 0)
        for z in range(nz):
            store(chunk, z).start()

    for away in range(1, n_det):

        @pl.when(det - away >= 0)
        def _():
            depth_copy(away).wait_send()

        @pl.when(det + away < n_det)
        def _():
            column_copy(away).wait_send()

    for away in range(1, n_beam):
        beam_copy(away).wait_send()
    for away in range(n_beam):
        for part in (1, 0, 2):
            if part == 1 and away == 0:
                continue
            line_copy(part, away).wait_send()
    for away in range(1, n_slab):
        slab_copy(away, False).wait_send()
    for chunk in range(CHUNKS):
        for z in range(nz):
            store(chunk, z).wait()


def solution(mesh):
    sizes = (mesh.shape["beam"], mesh.shape["det"], mesh.shape["slab"])
    n_beam, n_det, n_slab = sizes

    def shards(concentration, cross_section, line_attenuation, energy_index, fan_offset, fan_weight, measured):
        n_s, nz, nx, ny = concentration.shape
        n_e, n_k = measured.shape[0], measured.shape[1]
        share = n_k // (n_beam * n_slab)
        volume = pltpu.VMEM((n_e, nx, nz, ny), F32)
        compact = (nx * nz // 128, 128)
        dma = pltpu.SemaphoreType.DMA
        scratch = [
            pltpu.VMEM((n_s, nx, nz, ny), F32),
            volume,
            volume,
            pltpu.VMEM((nx, nz, ny), F32),
            pltpu.VMEM((nx // BLOCK, BLOCK * nz, 2 * ny), BF16),
            pltpu.VMEM((n_e, n_k, ny), F32),
            pltpu.VMEM(((n_slab + 2) * nz, n_k), F32),
            pltpu.VMEM((3 * nz, n_k), F32),
            pltpu.VMEM((n_k, 128), F32),
            pltpu.VMEM((2 * REACH + 1, nz, ny), F32),
            pltpu.VMEM((n_e, nz, ny), F32),
            pltpu.VMEM((n_e, nz, ny), F32),
            pltpu.VMEM(compact, F32),
            pltpu.VMEM((n_det, *compact), F32),
            pltpu.VMEM((n_e, nz, ny), F32),
            pltpu.VMEM((n_beam, n_e, nz, ny), F32),
            pltpu.VMEM((n_beam, n_e, 3 * nz, ny), F32),
            pltpu.VMEM((n_e, 3 * nz, ny), F32),
            pltpu.VMEM((n_e, n_slab * nz, ny), F32),
            pltpu.VMEM(compact, F32),
            pltpu.VMEM((n_det, *compact), F32),
            dma((CHUNKS, nz)),
            dma,
            dma((n_det,)),
            dma((n_det,)),
            dma((n_beam,)),
            dma((n_beam,)),
            dma((3, n_beam)),
            dma((3, n_beam)),
            dma((n_slab,)),
            dma((n_slab,)),
            dma((n_det,)),
            dma((n_det,)),
            dma((CHUNKS, nz)),
        ]
        smem = pl.BlockSpec(memory_space=pltpu.SMEM)
        vmem = pl.BlockSpec(memory_space=pltpu.VMEM)
        anywhere = pl.BlockSpec(memory_space=pl.ANY)
        return pl.pallas_call(
            functools.partial(kernel, sizes),
            out_shape=(
                jax.ShapeDtypeStruct(concentration.shape, F32),
                jax.ShapeDtypeStruct((n_e, share, ny), F32),
            ),
            in_specs=[anywhere, smem, smem, smem, vmem, vmem, anywhere],
            out_specs=(anywhere, vmem),
            scratch_shapes=scratch,
            compiler_params=pltpu.CompilerParams(
                collective_id=0, has_side_effects=True, vmem_limit_bytes=48 * 2**20
            ),
        )(
            concentration,
            cross_section,
            line_attenuation,
            energy_index,
            fan_offset.reshape(1, n_k),
            fan_weight.T,
            measured,
        )

    in_specs = (P(None, "slab", "beam", "det"), P(), P(), P(), P(), P(), P(None, None, "det"))
    out_specs = (P(None, "slab", "beam", "det"), P(None, ("beam", "slab"), "det"))
    return jax.shard_map(shards, mesh=mesh, in_specs=in_specs, out_specs=out_specs, check_vma=False)
```

```python
import functools

import jax
import jax.numpy as jnp
from jax import lax
from jax.experimental import pallas as pl
from jax.experimental.pallas import tpu as pltpu
from jax.sharding import PartitionSpec as P

MESH = pl.DeviceIdType.MESH
F32 = jnp.float32
BF16 = jnp.bfloat16
HIGHEST = lax.Precision.HIGHEST
CHUNKS = 4
BLOCK = 16
REACH = 3


def split_pair(value):
    high = value.astype(BF16)
    low = (value - high.astype(F32)).astype(BF16)
    return jnp.concatenate([high, low], axis=1)


def row_totals(pair):
    ones = jnp.ones((8, pair.shape[1]), BF16)
    total = lax.dot_general(ones, pair, (((1,), (1,)), ((), ())), preferred_element_type=F32)
    return total[0:1]


def spread(compact):
    rows = compact.shape[0]
    padded = jnp.concatenate([compact, jnp.zeros((128 - rows, 128), F32)], axis=0)
    turned = jnp.transpose(padded)
    return [jnp.broadcast_to(turned[:, r : r + 1], (128, 128)) for r in range(rows)]


def kernel(
    sizes, conc, cross_in, lam_in, index_in, offset_in, weight_in, measured, part_out, near_out, lam_out, resid,
    cross, lam, index, offset, weight, c_buf, em, inc, dmp, hl, meas, wt, wx, wk, band, wm, up_buf,
    ra_send, ra_recv, ud_send, ud_recv, x_buf, xl, la, rc_send, rc_recv,
    in_sem, small_sem, meas_sem, ra_ss, ra_rs, ud_ss, ud_rs, x_ss, x_rs, la_ss, la_rs, rc_ss, rc_rs,
):
    n_beam, n_det, n_slab = sizes
    n_s, nz, nx, ny = conc.shape
    n_e = measured.shape[0]
    n_k = measured.shape[1]
    fan = weight_in.shape[0]
    c1 = 1.5 / (nx * n_beam)
    c2 = 1.5 / (ny * n_det)
    blocks = nx // BLOCK
    step = nx // CHUNKS
    per_chunk = blocks // CHUNKS
    beam, det, slab = lax.axis_index("beam"), lax.axis_index("det"), lax.axis_index("slab")

    def load(chunk, z):
        rows = pl.ds(chunk * step, step)
        return pltpu.make_async_copy(conc.at[:, z, rows, :], c_buf.at[:, rows, z, :], in_sem.at[chunk, z])

    pairs = ((cross_in, cross), (lam_in, lam), (index_in, index), (offset_in, offset), (weight_in, weight))
    small = [pltpu.make_async_copy(src, dst, small_sem.at[n]) for n, (src, dst) in enumerate(pairs)]
    for copy in small:
        copy.start()
    for chunk in range(CHUNKS):
        for z in range(nz):
            load(chunk, z).start()
    load_measured = pltpu.make_async_copy(measured, meas, meas_sem)
    load_measured.start()

    def beam_at(away):
        return lax.rem(beam + away, n_beam)

    def slab_at(away):
        return lax.rem(slab + away, n_slab)

    halo = (1, n_slab - 1)
    peers = [{"det": lax.rem(det + away, n_det)} for away in range(1, n_det)]
    for slab_away in range(n_slab):
        for beam_away in range(n_beam):
            if slab_away == 0 and beam_away == 0:
                continue
            if slab_away == 0 or slab_away in halo or beam_away == 0:
                peers.append({"beam": beam_at(beam_away), "slab": slab_at(slab_away)})
    barrier = pltpu.get_barrier_semaphore()
    for peer in peers:
        pl.semaphore_signal(barrier, inc=1, device_id=peer, device_id_type=MESH)

    def remote(src, dst, send, recv, device):
        return pltpu.make_async_remote_copy(
            src_ref=src, dst_ref=dst, send_sem=send, recv_sem=recv, device_id=device, device_id_type=MESH
        )

    def depth_copy(away):
        return remote(ra_send, ra_recv.at[away], ra_ss.at[away], ra_rs.at[away], {"det": lax.rem(det - away + n_det, n_det)})

    def column_copy(away):
        return remote(rc_send, rc_recv.at[away], rc_ss.at[away], rc_rs.at[away], {"det": lax.rem(det + away, n_det)})

    def beam_copy(away):
        slot = n_beam - away
        return remote(ud_send, ud_recv.at[slot], ud_ss.at[away], ud_rs.at[slot], {"beam": beam_at(away)})

    def line_copy(part, away):
        slot = (n_beam - away) % n_beam
        if part == 1:
            src, rows, target = x_buf.at[0, :, pl.ds(nz, nz), :], pl.ds(nz, nz), slab
        elif part == 0:
            src, rows, target = x_buf.at[0, :, pl.ds(2 * nz - REACH, REACH), :], pl.ds(nz - REACH, REACH), slab_at(1)
        else:
            src, rows, target = x_buf.at[0, :, pl.ds(nz, REACH), :], pl.ds(2 * nz, REACH), slab_at(n_slab - 1)
        return remote(
            src, x_buf.at[slot, :, rows, :], x_ss.at[part, away], x_rs.at[part, slot], {"beam": beam_at(away), "slab": target}
        )

    def slab_copy(away, receiving):
        source = slab_at(away) if receiving else slab
        rows = pl.ds(pl.multiple_of(source * nz, nz), nz)
        slot = away if receiving else n_slab - away
        return remote(
            xl.at[:, pl.ds(nz, nz), :], la.at[:, rows, :], la_ss.at[away], la_rs.at[slot], {"slab": slab_at(away)}
        )

    for copy in small:
        copy.wait()
    sigma = [[cross[s, index[e]] * c1 for e in range(n_e)] for s in range(n_s)]
    lam_near = [lam[s] * c2 for s in range(n_s)]
    lam_before = [lam[s] * (c2 / c1) for s in range(n_s)]

    def compact_totals(dst, low, high):
        total = row_totals(hl[low * step * nz : high * step * nz])
        for r in range(high * per_chunk - low * per_chunk):
            row = low * per_chunk + r
            dst[row : row + 1, :] = total[:, r * 128 : (r + 1) * 128]

    def first(block, depth):
        depth = list(depth)
        absorb = []
        for part in range(BLOCK // 4):
            rows = pl.ds(block * BLOCK + part * 4, 4)
            c = [c_buf[s, rows] for s in range(n_s)]
            ab = lam_near[0] * c[0]
            for s in range(1, n_s):
                ab = ab + lam_near[s] * c[s]
            absorb.append(ab)
            for e in range(n_e):
                value = sigma[0][e] * c[0]
                for s in range(1, n_s):
                    value = value + sigma[s][e] * c[s]
                em[e, rows] = value
                for x in range(4):
                    inc[e, block * BLOCK + part * 4 + x] = jnp.exp(depth[e])
                    depth[e] = depth[e] - value[x]
        hl[pl.ds(pl.multiple_of(block * BLOCK * nz, 128), BLOCK * nz)] = split_pair(
            jnp.concatenate(absorb, axis=0).reshape(BLOCK * nz, ny)
        )
        return tuple(depth)

    depth = (jnp.zeros((nz, ny), F32),) * n_e
    for chunk in range(CHUNKS):
        for z in range(nz):
            load(chunk, z).wait()
        depth = lax.fori_loop(chunk * per_chunk, (chunk + 1) * per_chunk, first, depth)
        if chunk % 2:
            compact_totals(ra_send, chunk - 1, chunk + 1)
    for e in range(n_e):
        ud_send[e] = depth[e]

    pl.semaphore_wait(barrier, len(peers))
    for away in range(1, n_det):

        @pl.when(det - away >= 0)
        def _():
            depth_copy(away).start()

    for away in range(1, n_beam):
        beam_copy(away).start()

    for away in range(1, n_det):

        @pl.when(det + away >= n_det)
        def _():
            ra_recv[away] = jnp.zeros_like(ra_send)

        @pl.when(det - away < 0)
        def _():
            rc_recv[away] = jnp.zeros_like(rc_send)

    deep = lax.broadcasted_iota(jnp.int32, (2 * ny, ny), 0) % ny
    wide = lax.broadcasted_iota(jnp.int32, (2 * ny, ny), 1)
    beyond = jnp.where(deep > wide, -1.0, 0.0).astype(BF16)
    nearer_side = jnp.where(deep < wide, 1.0, 0.0).astype(BF16)

    tile = BLOCK * nz
    for block in range(blocks):
        path = jnp.dot(hl[block * tile : (block + 1) * tile], beyond, preferred_element_type=F32)
        escape = jnp.exp(path).reshape(BLOCK, nz, ny)
        rows = pl.ds(block * BLOCK, BLOCK)
        for e in range(n_e):
            light = inc[e, rows] * escape
            inc[e, rows] = light
            em[e, rows] = em[e, rows] * light

    slices = lax.broadcasted_iota(jnp.int32, wt.shape, 0) - nz
    full = jnp.zeros(wt.shape, F32)
    for j in range(fan):
        tap = weight[j : j + 1, :].astype(F32)
        full = full + jnp.where(offset[...] + j == slices, tap, 0.0)
    wt[...] = full
    wx[...] = wt[pl.ds(pl.multiple_of(slab * nz, nz), 3 * nz), :]
    whole = wt[nz : nz + n_slab * nz, :]
    padded = jnp.concatenate([whole, jnp.zeros((128 - n_slab * nz, n_k), F32)], axis=0)
    wk[...] = jnp.transpose(padded)
    own = wx[nz : 2 * nz, :]
    for shift in range(2 * REACH + 1):
        other = wx[nz - REACH + shift : 2 * nz - REACH + shift, :]
        band[shift] = jnp.broadcast_to(jnp.sum(own * other, axis=1, keepdims=True), (nz, ny))
    load_measured.wait()
    for e in range(n_e):
        wm[e] = jnp.dot(own, meas[e], precision=HIGHEST, preferred_element_type=F32)

    for away in range(1, n_beam):
        beam_copy(away).wait_recv()
    upstream = jnp.zeros((n_e, nz, ny), F32)
    for slot in range(1, n_beam):
        upstream = upstream + jnp.where(beam + slot >= n_beam, 1.0, 0.0) * ud_recv[slot]
    up_buf[...] = jnp.exp(upstream)

    for away in range(1, n_det):

        @pl.when(det + away < n_det)
        def _():
            depth_copy(away).wait_recv()

    downstream = ra_recv[1]
    for away in range(2, n_det):
        downstream = downstream + ra_recv[away]
    for r, piece in enumerate(spread(jnp.exp(-downstream))):
        dmp[r * BLOCK : (r + 1) * BLOCK] = piece.reshape(BLOCK, nz, ny)

    def third(block, sums):
        rows = pl.ds(block * BLOCK, BLOCK)
        damp = dmp[rows]
        return tuple(sums[e] + jnp.sum(em[e, rows] * damp, axis=0) for e in range(n_e))

    sums = lax.fori_loop(0, blocks, third, (jnp.zeros((nz, ny), F32),) * n_e)
    for e in range(n_e):
        x_buf[0, e, nz : 2 * nz] = sums[e] * up_buf[e]
    for away in range(n_beam):
        for part in (1, 0, 2):
            if part == 1 and away == 0:
                continue
            line_copy(part, away).start()

    def fourth(count, after):
        block = blocks - 1 - count
        after = list(after)
        for x in range(BLOCK - 1, -1, -1):
            row = block * BLOCK + x
            damp = dmp[row]
            for e in range(n_e):
                fluor = em[e, row] * damp
                inc[e, row] = inc[e, row] * damp - after[e]
                em[e, row] = fluor
                after[e] = after[e] + fluor
        return tuple(after)

    lax.fori_loop(0, blocks, fourth, (jnp.zeros((nz, ny), F32),) * n_e)

    for away in range(n_beam):
        for part in (1, 0, 2):
            if part == 1 and away == 0:
                continue
            line_copy(part, away).wait_recv()
    near = slice(nz - REACH, 2 * nz + REACH)
    extent = x_buf[0, :, near]
    for slot in range(1, n_beam):
        extent = extent + x_buf[slot, :, near]
    xl[:, near] = extent
    further = jnp.zeros((n_e, nz, ny), F32)
    for slot in range(1, n_beam):
        further = further + jnp.where(beam + slot < n_beam, 1.0, 0.0) * x_buf[slot, :, nz : 2 * nz]
    back = []
    for e in range(n_e):
        value = band[0] * xl[e, nz - REACH : 2 * nz - REACH]
        for shift in range(1, 2 * REACH + 1):
            value = value + band[shift] * xl[e, nz - REACH + shift : 2 * nz - REACH + shift]
        back.append(value * (1.0 / 1.5) - wm[e])
    lit = [back[e] * up_buf[e] for e in range(n_e)]

    for block in range(blocks):
        rows = pl.ds(block * BLOCK, BLOCK)
        heavy = lit[0] * em[0, rows]
        for e in range(1, n_e):
            heavy = heavy + lit[e] * em[e, rows]
        pair = split_pair(heavy.reshape(tile, ny))
        hl[block * tile : (block + 1) * tile] = pair
        rc_send[block : block + 1, :] = row_totals(pair)
    for away in range(1, n_det):

        @pl.when(det + away < n_det)
        def _():
            column_copy(away).start()

    for away in range(1, n_slab):
        slab_copy(away, False).start()
    la[:, pl.ds(pl.multiple_of(slab * nz, nz), nz), :] = xl[:, nz : 2 * nz, :]
    shade = [back[e] * further[e] for e in range(n_e)]
    mix, less = [], []
    for s in range(n_s):
        pull = [cross[s, index[e]] for e in range(n_e)]
        mix.append([pull[e] * lit[e] for e in range(n_e)])
        value = pull[0] * shade[0]
        for e in range(1, n_e):
            value = value + pull[e] * shade[e]
        less.append(value)

    for block in range(blocks):
        before = jnp.dot(hl[block * tile : (block + 1) * tile], nearer_side, preferred_element_type=F32)
        dmp[block * BLOCK : (block + 1) * BLOCK] = before.reshape(BLOCK, nz, ny)

    def sixth(block, carry):
        for part in range(BLOCK // 4):
            rows = pl.ds(block * BLOCK + part * 4, 4)
            term = [inc[e, rows] for e in range(n_e)]
            for s in range(n_s):
                value = mix[s][0] * term[0]
                for e in range(1, n_e):
                    value = value + mix[s][e] * term[e]
                part_out[s, rows] = value - less[s] - lam_before[s] * dmp[rows]
        return carry

    lax.fori_loop(0, blocks, sixth, 0)

    for away in range(1, n_slab):
        slab_copy(away, True).wait_recv()
    share = n_k // (n_beam * n_slab)
    mine = pl.ds(pl.multiple_of((beam * n_slab + slab) * share, share), share)
    for e in range(n_e):
        signal = jnp.dot(wk[mine, 0 : n_slab * nz], la[e], precision=HIGHEST, preferred_element_type=F32)
        resid[e] = signal * (1.0 / 1.5) - meas[e, mine]

    for away in range(1, n_det):

        @pl.when(det - away >= 0)
        def _():
            remote(rc_send, rc_recv.at[away], rc_ss.at[away], rc_rs.at[away], {"det": lax.rem(det + away, n_det)}).wait_recv()

    nearer = rc_recv[1]
    for away in range(2, n_det):
        nearer = nearer + rc_recv[away]
    near_out[...] = nearer
    for s in range(n_s):
        lam_out[s] = jnp.full((nz, ny), lam_before[s], F32)

    for away in range(1, n_det):

        @pl.when(det - away >= 0)
        def _():
            depth_copy(away).wait_send()

        @pl.when(det + away < n_det)
        def _():
            column_copy(away).wait_send()

    for away in range(1, n_beam):
        beam_copy(away).wait_send()
    for away in range(n_beam):
        for part in (1, 0, 2):
            if part == 1 and away == 0:
                continue
            line_copy(part, away).wait_send()
    for away in range(1, n_slab):
        slab_copy(away, False).wait_send()


def finish(part, near, lam_before, resid_in, out, resid, buf, out_sem):
    n_s, nx, nz, ny = part.shape
    step = nx // CHUNKS
    resid[...] = resid_in[...]
    pieces = spread(near[...])

    def store(chunk, z):
        rows = pl.ds(chunk * step, step)
        return pltpu.make_async_copy(buf.at[:, rows, z, :], out.at[:, z, rows, :], out_sem.at[chunk, z])

    for chunk in range(CHUNKS):
        for block in range(chunk * step // BLOCK, (chunk + 1) * step // BLOCK):
            rows = slice(block * BLOCK, (block + 1) * BLOCK)
            shift = pieces[block].reshape(BLOCK, nz, ny)
            for s in range(n_s):
                buf[s, rows] = part[s, rows] - lam_before[s] * shift
        for z in range(nz):
            store(chunk, z).start()
    for chunk in range(CHUNKS):
        for z in range(nz):
            store(chunk, z).wait()


def solution(mesh):
    sizes = (mesh.shape["beam"], mesh.shape["det"], mesh.shape["slab"])
    n_beam, n_det, n_slab = sizes

    def shards(concentration, cross_section, line_attenuation, energy_index, fan_offset, fan_weight, measured):
        n_s, nz, nx, ny = concentration.shape
        n_e, n_k = measured.shape[0], measured.shape[1]
        share = n_k // (n_beam * n_slab)
        volume = pltpu.VMEM((n_e, nx, nz, ny), F32)
        compact = (nx * nz // 128, 128)
        dma = pltpu.SemaphoreType.DMA
        scratch = [
            pltpu.SMEM(cross_section.shape, F32),
            pltpu.SMEM(line_attenuation.shape, F32),
            pltpu.SMEM(energy_index.shape, jnp.int32),
            pltpu.VMEM((1, n_k), jnp.int32),
            pltpu.VMEM((fan_weight.shape[1], n_k), jnp.int32),
            pltpu.VMEM((n_s, nx, nz, ny), F32),
            volume,
            volume,
            pltpu.VMEM((nx, nz, ny), F32),
            pltpu.VMEM((nx * nz, 2 * ny), BF16),
            pltpu.VMEM((n_e, n_k, ny), F32),
            pltpu.VMEM(((n_slab + 2) * nz, n_k), F32),
            pltpu.VMEM((3 * nz, n_k), F32),
            pltpu.VMEM((n_k, 128), F32),
            pltpu.VMEM((2 * REACH + 1, nz, ny), F32),
            pltpu.VMEM((n_e, nz, ny), F32),
            pltpu.VMEM((n_e, nz, ny), F32),
            pltpu.VMEM(compact, F32),
            pltpu.VMEM((n_det, *compact), F32),
            pltpu.VMEM((n_e, nz, ny), F32),
            pltpu.VMEM((n_beam, n_e, nz, ny), F32),
            pltpu.VMEM((n_beam, n_e, 3 * nz, ny), F32),
            pltpu.VMEM((n_e, 3 * nz, ny), F32),
            pltpu.VMEM((n_e, n_slab * nz, ny), F32),
            pltpu.VMEM(compact, F32),
            pltpu.VMEM((n_det, *compact), F32),
            dma((CHUNKS, nz)),
            dma((5,)),
            dma,
            dma((n_det,)),
            dma((n_det,)),
            dma((n_beam,)),
            dma((n_beam,)),
            dma((3, n_beam)),
            dma((3, n_beam)),
            dma((n_slab,)),
            dma((n_slab,)),
            dma((n_det,)),
            dma((n_det,)),
        ]
        hbm = pl.BlockSpec(memory_space=pltpu.HBM)
        vmem = pl.BlockSpec(memory_space=pltpu.VMEM)
        share_shape = (n_e, share, ny)
        passed = pl.pallas_call(
            functools.partial(kernel, sizes),
            out_shape=(
                pltpu.VMEM((n_s, nx, nz, ny), F32),
                pltpu.VMEM(compact, F32),
                pltpu.VMEM((n_s, nz, ny), F32),
                pltpu.VMEM(share_shape, F32),
            ),
            in_specs=[hbm] * 7,
            out_specs=(vmem,) * 4,
            scratch_shapes=scratch,
            compiler_params=pltpu.CompilerParams(
                collective_id=0, has_side_effects=True, vmem_limit_bytes=28 * 2**20
            ),
        )(
            *(
                pltpu.with_memory_space_constraint(array, pltpu.HBM)
                for array in (
                    concentration,
                    cross_section,
                    line_attenuation,
                    energy_index,
                    fan_offset.reshape(1, n_k),
                    fan_weight.T,
                    measured,
                )
            )
        )
        return pl.pallas_call(
            finish,
            out_shape=(
                jax.ShapeDtypeStruct(concentration.shape, F32),
                jax.ShapeDtypeStruct(share_shape, F32),
            ),
            in_specs=[vmem] * 4,
            out_specs=(hbm, vmem),
            scratch_shapes=[pltpu.VMEM((n_s, nx, nz, ny), F32), dma((CHUNKS, nz))],
            compiler_params=pltpu.CompilerParams(vmem_limit_bytes=16 * 2**20),
        )(*passed)

    in_specs = (P(None, "slab", "beam", "det"), P(), P(), P(), P(), P(), P(None, None, "det"))
    out_specs = (P(None, "slab", "beam", "det"), P(None, ("beam", "slab"), "det"))
    return jax.shard_map(shards, mesh=mesh, in_specs=in_specs, out_specs=out_specs, check_vma=False)
```

```python
import functools

import jax
import jax.numpy as jnp
from jax import lax
from jax.experimental import pallas as pl
from jax.experimental.pallas import tpu as pltpu
from jax.sharding import PartitionSpec as P

MESH = pl.DeviceIdType.MESH
F32 = jnp.float32
BF16 = jnp.bfloat16
HIGHEST = lax.Precision.HIGHEST
CHUNKS = 2
STORES = 4
BLOCK = 16
REACH = 3


def split_pair(value):
    high = value.astype(BF16)
    low = (value - high.astype(F32)).astype(BF16)
    return jnp.concatenate([high, low], axis=1)


def row_totals(pair):
    ones = jnp.ones((8, pair.shape[1]), BF16)
    total = lax.dot_general(ones, pair, (((1,), (1,)), ((), ())), preferred_element_type=F32)
    return total[0:1]


def spread(compact):
    rows = compact.shape[0]
    padded = jnp.concatenate([compact, jnp.zeros((128 - rows, 128), F32)], axis=0)
    turned = jnp.transpose(padded)
    return [jnp.broadcast_to(turned[:, r : r + 1], (128, 128)) for r in range(rows)]


def kernel(
    sizes, conc, cross_in, lam_in, index_in, offset_in, weight_in, measured, part_out, near_out, lam_out, resid,
    cross, lam, index, offset, weight, c_buf, em, inc, dmp, hl, meas, wt, wx, wk, band, wm, up_buf,
    ra_send, ra_recv, ud_send, ud_recv, x_buf, xl, la, rc_send, rc_recv,
    in_sem, small_sem, meas_sem, ra_ss, ra_rs, ud_ss, ud_rs, x_ss, x_rs, la_ss, la_rs, rc_ss, rc_rs,
):
    n_beam, n_det, n_slab = sizes
    n_s, nz, nx, ny = conc.shape
    n_e = measured.shape[0]
    n_k = measured.shape[1]
    fan = weight_in.shape[0]
    c1 = 1.5 / (nx * n_beam)
    c2 = 1.5 / (ny * n_det)
    blocks = nx // BLOCK
    step = nx // CHUNKS
    per_chunk = blocks // CHUNKS
    beam, det, slab = lax.axis_index("beam"), lax.axis_index("det"), lax.axis_index("slab")

    def load(chunk, z):
        rows = pl.ds(chunk * step, step)
        return pltpu.make_async_copy(conc.at[:, z, rows, :], c_buf.at[:, rows, z, :], in_sem.at[chunk, z])

    pairs = ((cross_in, cross), (lam_in, lam), (index_in, index), (offset_in, offset), (weight_in, weight))
    small = [pltpu.make_async_copy(src, dst, small_sem.at[n]) for n, (src, dst) in enumerate(pairs)]
    for copy in small:
        copy.start()
    for chunk in range(CHUNKS):
        for z in range(nz):
            load(chunk, z).start()
    load_measured = pltpu.make_async_copy(measured, meas, meas_sem)
    load_measured.start()

    def beam_at(away):
        return lax.rem(beam + away, n_beam)

    def slab_at(away):
        return lax.rem(slab + away, n_slab)

    halo = (1, n_slab - 1)
    peers = [{"det": lax.rem(det + away, n_det)} for away in range(1, n_det)]
    for slab_away in range(n_slab):
        for beam_away in range(n_beam):
            if slab_away == 0 and beam_away == 0:
                continue
            if slab_away == 0 or slab_away in halo or beam_away == 0:
                peers.append({"beam": beam_at(beam_away), "slab": slab_at(slab_away)})
    barrier = pltpu.get_barrier_semaphore()
    for peer in peers:
        pl.semaphore_signal(barrier, inc=1, device_id=peer, device_id_type=MESH)

    def remote(src, dst, send, recv, device):
        return pltpu.make_async_remote_copy(
            src_ref=src, dst_ref=dst, send_sem=send, recv_sem=recv, device_id=device, device_id_type=MESH
        )

    def depth_copy(away):
        return remote(ra_send, ra_recv.at[away], ra_ss.at[away], ra_rs.at[away], {"det": lax.rem(det - away + n_det, n_det)})

    def column_copy(away):
        return remote(rc_send, rc_recv.at[away], rc_ss.at[away], rc_rs.at[away], {"det": lax.rem(det + away, n_det)})

    def beam_copy(away):
        slot = n_beam - away
        return remote(ud_send, ud_recv.at[slot], ud_ss.at[away], ud_rs.at[slot], {"beam": beam_at(away)})

    def line_copy(part, away):
        slot = (n_beam - away) % n_beam
        if part == 1:
            src, rows, target = x_buf.at[0, :, pl.ds(nz, nz), :], pl.ds(nz, nz), slab
        elif part == 0:
            src, rows, target = x_buf.at[0, :, pl.ds(2 * nz - REACH, REACH), :], pl.ds(nz - REACH, REACH), slab_at(1)
        else:
            src, rows, target = x_buf.at[0, :, pl.ds(nz, REACH), :], pl.ds(2 * nz, REACH), slab_at(n_slab - 1)
        return remote(
            src, x_buf.at[slot, :, rows, :], x_ss.at[part, away], x_rs.at[part, slot], {"beam": beam_at(away), "slab": target}
        )

    order = sorted(range(n_beam), key=lambda away: abs(2 * away - n_beam))
    lines = [(part, away) for away in order for part in (0, 2)] + [(1, away) for away in order if away]

    def slab_copy(away, receiving):
        source = slab_at(away) if receiving else slab
        rows = pl.ds(pl.multiple_of(source * nz, nz), nz)
        slot = away if receiving else n_slab - away
        return remote(
            xl.at[:, pl.ds(nz, nz), :], la.at[:, rows, :], la_ss.at[away], la_rs.at[slot], {"slab": slab_at(away)}
        )

    for copy in small:
        copy.wait()
    sigma = [[cross[s, index[e]] * c1 for e in range(n_e)] for s in range(n_s)]
    lam_near = [lam[s] * c2 for s in range(n_s)]
    lam_before = [lam[s] * (c2 / c1) for s in range(n_s)]

    tile = BLOCK * nz

    def totals_of(value, block, dst):
        pair = split_pair(value.reshape(tile, ny))
        hl[block * tile : (block + 1) * tile] = pair
        dst[block : block + 1, :] = row_totals(pair)

    for chunk in range(CHUNKS):
        for z in range(nz):
            load(chunk, z).wait()
        for block in range(chunk * per_chunk, (chunk + 1) * per_chunk):
            rows = pl.ds(block * BLOCK, BLOCK)
            absorb = lam_near[0] * c_buf[0, rows]
            for s in range(1, n_s):
                absorb = absorb + lam_near[s] * c_buf[s, rows]
            totals_of(absorb, block, ra_send)
    pl.semaphore_wait(barrier, len(peers))
    for away in range(1, n_det):

        @pl.when(det - away >= 0)
        def _():
            depth_copy(away).start()

    def first(block, depth):
        depth = list(depth)
        for part in range(BLOCK // 4):
            rows = pl.ds(block * BLOCK + part * 4, 4)
            c = [c_buf[s, rows] for s in range(n_s)]
            for e in range(n_e):
                value = sigma[0][e] * c[0]
                for s in range(1, n_s):
                    value = value + sigma[s][e] * c[s]
                em[e, rows] = value
                for x in range(4):
                    inc[e, block * BLOCK + part * 4 + x] = jnp.exp(depth[e])
                    depth[e] = depth[e] - value[x]
        return tuple(depth)

    depth = lax.fori_loop(0, blocks, first, (jnp.zeros((nz, ny), F32),) * n_e)
    for e in range(n_e):
        ud_send[e] = depth[e]
    for away in range(1, n_beam):
        beam_copy(away).start()

    for away in range(1, n_det):

        @pl.when(det + away >= n_det)
        def _():
            ra_recv[away] = jnp.zeros_like(ra_send)

        @pl.when(det - away < 0)
        def _():
            rc_recv[away] = jnp.zeros_like(rc_send)

    deep = lax.broadcasted_iota(jnp.int32, (2 * ny, ny), 0) % ny
    wide = lax.broadcasted_iota(jnp.int32, (2 * ny, ny), 1)
    beyond = jnp.where(deep > wide, -1.0, 0.0).astype(BF16)
    nearer_side = jnp.where(deep < wide, 1.0, 0.0).astype(BF16)

    for block in range(blocks):
        path = jnp.dot(hl[block * tile : (block + 1) * tile], beyond, preferred_element_type=F32)
        escape = jnp.exp(path).reshape(BLOCK, nz, ny)
        rows = pl.ds(block * BLOCK, BLOCK)
        for e in range(n_e):
            light = inc[e, rows] * escape
            inc[e, rows] = light
            em[e, rows] = em[e, rows] * light

    slices = lax.broadcasted_iota(jnp.int32, wt.shape, 0) - nz
    full = jnp.zeros(wt.shape, F32)
    for j in range(fan):
        tap = weight[j : j + 1, :].astype(F32)
        full = full + jnp.where(offset[...] + j == slices, tap, 0.0)
    wt[...] = full
    wx[...] = wt[pl.ds(pl.multiple_of(slab * nz, nz), 3 * nz), :]
    whole = wt[nz : nz + n_slab * nz, :]
    padded = jnp.concatenate([whole, jnp.zeros((128 - n_slab * nz, n_k), F32)], axis=0)
    wk[...] = jnp.transpose(padded)
    own = wx[nz : 2 * nz, :]
    for shift in range(2 * REACH + 1):
        other = wx[nz - REACH + shift : 2 * nz - REACH + shift, :]
        band[shift] = jnp.broadcast_to(jnp.sum(own * other, axis=1, keepdims=True), (nz, ny))
    load_measured.wait()
    for e in range(n_e):
        wm[e] = jnp.dot(own, meas[e], precision=HIGHEST, preferred_element_type=F32)

    for away in range(1, n_beam):
        beam_copy(away).wait_recv()
    upstream = jnp.zeros((n_e, nz, ny), F32)
    for slot in range(1, n_beam):
        upstream = upstream + jnp.where(beam + slot >= n_beam, 1.0, 0.0) * ud_recv[slot]
    up_buf[...] = jnp.exp(upstream)

    for away in range(1, n_det):

        @pl.when(det + away < n_det)
        def _():
            depth_copy(away).wait_recv()

    downstream = ra_recv[1]
    for away in range(2, n_det):
        downstream = downstream + ra_recv[away]
    for r, piece in enumerate(spread(jnp.exp(-downstream))):
        dmp[r * BLOCK : (r + 1) * BLOCK] = piece.reshape(BLOCK, nz, ny)

    def third(block, sums):
        rows = pl.ds(block * BLOCK, BLOCK)
        damp = dmp[rows]
        return tuple(sums[e] + jnp.sum(em[e, rows] * damp, axis=0) for e in range(n_e))

    sums = lax.fori_loop(0, blocks, third, (jnp.zeros((nz, ny), F32),) * n_e)
    for e in range(n_e):
        x_buf[0, e, nz : 2 * nz] = sums[e] * up_buf[e]
    for part, away in lines:
        line_copy(part, away).start()

    def fourth(count, after):
        block = blocks - 1 - count
        after = list(after)
        for x in range(BLOCK - 1, -1, -1):
            row = block * BLOCK + x
            damp = dmp[row]
            for e in range(n_e):
                fluor = em[e, row] * damp
                inc[e, row] = inc[e, row] * damp - after[e]
                em[e, row] = fluor
                after[e] = after[e] + fluor
        return tuple(after)

    lax.fori_loop(0, blocks, fourth, (jnp.zeros((nz, ny), F32),) * n_e)

    for part, away in lines:
        line_copy(part, away).wait_recv()
    near = slice(nz - REACH, 2 * nz + REACH)
    extent = x_buf[0, :, near]
    for slot in range(1, n_beam):
        extent = extent + x_buf[slot, :, near]
    xl[:, near] = extent
    further = jnp.zeros((n_e, nz, ny), F32)
    for slot in range(1, n_beam):
        further = further + jnp.where(beam + slot < n_beam, 1.0, 0.0) * x_buf[slot, :, nz : 2 * nz]
    back = []
    for e in range(n_e):
        value = band[0] * xl[e, nz - REACH : 2 * nz - REACH]
        for shift in range(1, 2 * REACH + 1):
            value = value + band[shift] * xl[e, nz - REACH + shift : 2 * nz - REACH + shift]
        back.append(value * (1.0 / 1.5) - wm[e])
    lit = [back[e] * up_buf[e] for e in range(n_e)]

    for block in range(blocks):
        rows = pl.ds(block * BLOCK, BLOCK)
        heavy = lit[0] * em[0, rows]
        for e in range(1, n_e):
            heavy = heavy + lit[e] * em[e, rows]
        totals_of(heavy, block, rc_send)
    for away in range(1, n_det):

        @pl.when(det + away < n_det)
        def _():
            column_copy(away).start()

    for away in range(1, n_slab):
        slab_copy(away, False).start()
    la[:, pl.ds(pl.multiple_of(slab * nz, nz), nz), :] = xl[:, nz : 2 * nz, :]
    shade = [back[e] * further[e] for e in range(n_e)]
    mix, less = [], []
    for s in range(n_s):
        pull = [cross[s, index[e]] for e in range(n_e)]
        mix.append([pull[e] * lit[e] for e in range(n_e)])
        value = pull[0] * shade[0]
        for e in range(1, n_e):
            value = value + pull[e] * shade[e]
        less.append(value)

    for block in range(blocks):
        before = jnp.dot(hl[block * tile : (block + 1) * tile], nearer_side, preferred_element_type=F32)
        dmp[block * BLOCK : (block + 1) * BLOCK] = before.reshape(BLOCK, nz, ny)

    def sixth(block, carry):
        for part in range(BLOCK // 4):
            rows = pl.ds(block * BLOCK + part * 4, 4)
            term = [inc[e, rows] for e in range(n_e)]
            for s in range(n_s):
                value = mix[s][0] * term[0]
                for e in range(1, n_e):
                    value = value + mix[s][e] * term[e]
                part_out[s, rows] = value - less[s] - lam_before[s] * dmp[rows]
        return carry

    lax.fori_loop(0, blocks, sixth, 0)

    for away in range(1, n_slab):
        slab_copy(away, True).wait_recv()
    share = n_k // (n_beam * n_slab)
    mine = pl.ds(pl.multiple_of((beam * n_slab + slab) * share, share), share)
    for e in range(n_e):
        signal = jnp.dot(wk[mine, 0 : n_slab * nz], la[e], precision=HIGHEST, preferred_element_type=F32)
        resid[e] = signal * (1.0 / 1.5) - meas[e, mine]

    for away in range(1, n_det):

        @pl.when(det - away >= 0)
        def _():
            remote(rc_send, rc_recv.at[away], rc_ss.at[away], rc_rs.at[away], {"det": lax.rem(det + away, n_det)}).wait_recv()

    nearer = rc_recv[1]
    for away in range(2, n_det):
        nearer = nearer + rc_recv[away]
    near_out[...] = nearer
    for s in range(n_s):
        lam_out[s] = jnp.full((nz, ny), lam_before[s], F32)

    for away in range(1, n_det):

        @pl.when(det - away >= 0)
        def _():
            depth_copy(away).wait_send()

        @pl.when(det + away < n_det)
        def _():
            column_copy(away).wait_send()

    for away in range(1, n_beam):
        beam_copy(away).wait_send()
    for part, away in lines:
        line_copy(part, away).wait_send()
    for away in range(1, n_slab):
        slab_copy(away, False).wait_send()


def finish(part, near, lam_before, resid_in, out, resid, buf, out_sem):
    n_s, nx, nz, ny = part.shape
    step = nx // STORES
    resid[...] = resid_in[...]
    pieces = spread(near[...])

    def store(chunk, z):
        rows = pl.ds(chunk * step, step)
        return pltpu.make_async_copy(buf.at[:, rows, z, :], out.at[:, z, rows, :], out_sem.at[chunk, z])

    for chunk in range(STORES):
        for block in range(chunk * step // BLOCK, (chunk + 1) * step // BLOCK):
            rows = slice(block * BLOCK, (block + 1) * BLOCK)
            shift = pieces[block].reshape(BLOCK, nz, ny)
            for s in range(n_s):
                buf[s, rows] = part[s, rows] - lam_before[s] * shift
        for z in range(nz):
            store(chunk, z).start()
    for chunk in range(STORES):
        for z in range(nz):
            store(chunk, z).wait()


def solution(mesh):
    sizes = (mesh.shape["beam"], mesh.shape["det"], mesh.shape["slab"])
    n_beam, n_det, n_slab = sizes

    def shards(concentration, cross_section, line_attenuation, energy_index, fan_offset, fan_weight, measured):
        n_s, nz, nx, ny = concentration.shape
        n_e, n_k = measured.shape[0], measured.shape[1]
        share = n_k // (n_beam * n_slab)
        volume = pltpu.VMEM((n_e, nx, nz, ny), F32)
        compact = (nx * nz // 128, 128)
        dma = pltpu.SemaphoreType.DMA
        scratch = [
            pltpu.SMEM(cross_section.shape, F32),
            pltpu.SMEM(line_attenuation.shape, F32),
            pltpu.SMEM(energy_index.shape, jnp.int32),
            pltpu.VMEM((1, n_k), jnp.int32),
            pltpu.VMEM((fan_weight.shape[1], n_k), jnp.int32),
            pltpu.VMEM((n_s, nx, nz, ny), F32),
            volume,
            volume,
            pltpu.VMEM((nx, nz, ny), F32),
            pltpu.VMEM((nx * nz, 2 * ny), BF16),
            pltpu.VMEM((n_e, n_k, ny), F32),
            pltpu.VMEM(((n_slab + 2) * nz, n_k), F32),
            pltpu.VMEM((3 * nz, n_k), F32),
            pltpu.VMEM((n_k, 128), F32),
            pltpu.VMEM((2 * REACH + 1, nz, ny), F32),
            pltpu.VMEM((n_e, nz, ny), F32),
            pltpu.VMEM((n_e, nz, ny), F32),
            pltpu.VMEM(compact, F32),
            pltpu.VMEM((n_det, *compact), F32),
            pltpu.VMEM((n_e, nz, ny), F32),
            pltpu.VMEM((n_beam, n_e, nz, ny), F32),
            pltpu.VMEM((n_beam, n_e, 3 * nz, ny), F32),
            pltpu.VMEM((n_e, 3 * nz, ny), F32),
            pltpu.VMEM((n_e, n_slab * nz, ny), F32),
            pltpu.VMEM(compact, F32),
            pltpu.VMEM((n_det, *compact), F32),
            dma((STORES, nz)),
            dma((5,)),
            dma,
            dma((n_det,)),
            dma((n_det,)),
            dma((n_beam,)),
            dma((n_beam,)),
            dma((3, n_beam)),
            dma((3, n_beam)),
            dma((n_slab,)),
            dma((n_slab,)),
            dma((n_det,)),
            dma((n_det,)),
        ]
        hbm = pl.BlockSpec(memory_space=pltpu.HBM)
        vmem = pl.BlockSpec(memory_space=pltpu.VMEM)
        share_shape = (n_e, share, ny)
        passed = pl.pallas_call(
            functools.partial(kernel, sizes),
            out_shape=(
                pltpu.VMEM((n_s, nx, nz, ny), F32),
                pltpu.VMEM(compact, F32),
                pltpu.VMEM((n_s, nz, ny), F32),
                pltpu.VMEM(share_shape, F32),
            ),
            in_specs=[hbm] * 7,
            out_specs=(vmem,) * 4,
            scratch_shapes=scratch,
            compiler_params=pltpu.CompilerParams(
                collective_id=0, has_side_effects=True, vmem_limit_bytes=28 * 2**20
            ),
        )(
            *(
                pltpu.with_memory_space_constraint(array, pltpu.HBM)
                for array in (
                    concentration,
                    cross_section,
                    line_attenuation,
                    energy_index,
                    fan_offset.reshape(1, n_k),
                    fan_weight.T,
                    measured,
                )
            )
        )
        return pl.pallas_call(
            finish,
            out_shape=(
                jax.ShapeDtypeStruct(concentration.shape, F32),
                jax.ShapeDtypeStruct(share_shape, F32),
            ),
            in_specs=[vmem] * 4,
            out_specs=(hbm, vmem),
            scratch_shapes=[pltpu.VMEM((n_s, nx, nz, ny), F32), dma((STORES, nz))],
            compiler_params=pltpu.CompilerParams(vmem_limit_bytes=16 * 2**20),
        )(*passed)

    in_specs = (P(None, "slab", "beam", "det"), P(), P(), P(), P(), P(), P(None, None, "det"))
    out_specs = (P(None, "slab", "beam", "det"), P(None, ("beam", "slab"), "det"))
    return jax.shard_map(shards, mesh=mesh, in_specs=in_specs, out_specs=out_specs, check_vma=False)
```

```python
import functools

import jax
import jax.numpy as jnp
from jax import lax
from jax.experimental import pallas as pl
from jax.experimental.pallas import tpu as pltpu
from jax.sharding import PartitionSpec as P

MESH = pl.DeviceIdType.MESH
F32 = jnp.float32
BF16 = jnp.bfloat16
HIGHEST = lax.Precision.HIGHEST
CHUNKS = 2
STORES = 4
BLOCK = 16
REACH = 3


def split_pair(value):
    high = value.astype(BF16)
    low = (value - high.astype(F32)).astype(BF16)
    return jnp.concatenate([high, low], axis=1)


def row_totals(pair):
    ones = jnp.ones((8, pair.shape[1]), BF16)
    total = lax.dot_general(ones, pair, (((1,), (1,)), ((), ())), preferred_element_type=F32)
    return total[0:1]


def spread(compact):
    rows = compact.shape[0]
    padded = jnp.concatenate([compact, jnp.zeros((128 - rows, 128), F32)], axis=0)
    turned = jnp.transpose(padded)
    return [jnp.broadcast_to(turned[:, r : r + 1], (128, 128)) for r in range(rows)]


def kernel(
    sizes, conc, cross_in, lam_in, index_in, offset_in, weight_in, measured, part_out, near_out, lam_out, resid,
    cross, lam, index, offset, weight, c_buf, em, inc, dmp, hl, meas, wt, wx, wk, band, wm, up_buf,
    ra_send, ra_recv, ud_send, ud_recv, x_buf, xl, la, rc_send, rc_recv,
    in_sem, small_sem, meas_sem, ra_ss, ra_rs, ud_ss, ud_rs, x_ss, x_rs, la_ss, la_rs, rc_ss, rc_rs, relay_one, relay_two,
):
    n_beam, n_det, n_slab = sizes
    n_s, nz, nx, ny = conc.shape
    n_e = measured.shape[0]
    n_k = measured.shape[1]
    fan = weight_in.shape[0]
    c1 = 1.5 / (nx * n_beam)
    c2 = 1.5 / (ny * n_det)
    blocks = nx // BLOCK
    step = nx // CHUNKS
    per_chunk = blocks // CHUNKS
    beam, det, slab = lax.axis_index("beam"), lax.axis_index("det"), lax.axis_index("slab")

    def load(chunk, z):
        rows = pl.ds(chunk * step, step)
        return pltpu.make_async_copy(conc.at[:, z, rows, :], c_buf.at[:, rows, z, :], in_sem.at[chunk, z])

    pairs = ((cross_in, cross), (lam_in, lam), (index_in, index), (offset_in, offset), (weight_in, weight))
    small = [pltpu.make_async_copy(src, dst, small_sem.at[n]) for n, (src, dst) in enumerate(pairs)]
    for copy in small:
        copy.start()
    for chunk in range(CHUNKS):
        for z in range(nz):
            load(chunk, z).start()
    load_measured = pltpu.make_async_copy(measured, meas, meas_sem)
    load_measured.start()

    def beam_at(away):
        return lax.rem(beam + away, n_beam)

    def slab_at(away):
        return lax.rem(slab + away, n_slab)

    cores = 2
    deep_chips = n_beam // cores
    chips = deep_chips * n_slab
    chip, core = slab * deep_chips + beam // cores, lax.rem(beam, cores)

    def chip_at(away, core_at):
        there = lax.rem(chip + away, chips)
        return {"beam": lax.rem(there, deep_chips) * cores + core_at, "slab": there // deep_chips}

    near = [{"beam": beam - core + 1 - core}] + [chip_at(away, c) for away in (1, chips - 1) for c in range(cores)]
    barrier = pltpu.get_barrier_semaphore()
    for away in range(1, n_det):

        @pl.when(det + away < n_det)
        def _():
            pl.semaphore_signal(barrier, inc=1, device_id={"det": lax.rem(det + away, n_det)}, device_id_type=MESH)

    for peer in near:
        pl.semaphore_signal(barrier, inc=1, device_id=peer, device_id_type=MESH)

    def relay(sem):
        for away in (1, chips - 1):
            pl.semaphore_signal(sem, inc=1, device_id=chip_at(away, core), device_id_type=MESH)

    def remote(src, dst, send, recv, device):
        return pltpu.make_async_remote_copy(
            src_ref=src, dst_ref=dst, send_sem=send, recv_sem=recv, device_id=device, device_id_type=MESH
        )

    def depth_copy(away):
        return remote(ra_send, ra_recv.at[away], ra_ss.at[away], ra_rs.at[away], {"det": lax.rem(det - away + n_det, n_det)})

    def column_copy(away):
        return remote(rc_send, rc_recv.at[away], rc_ss.at[away], rc_rs.at[away], {"det": lax.rem(det + away, n_det)})

    def beam_copy(away):
        slot = n_beam - away
        return remote(ud_send, ud_recv.at[slot], ud_ss.at[away], ud_rs.at[slot], {"beam": beam_at(away)})

    def line_copy(part, away):
        slot = (n_beam - away) % n_beam
        if part == 1:
            src, rows, target = x_buf.at[0, :, pl.ds(nz, nz), :], pl.ds(nz, nz), slab
        elif part == 0:
            src, rows, target = x_buf.at[0, :, pl.ds(2 * nz - REACH, REACH), :], pl.ds(nz - REACH, REACH), slab_at(1)
        else:
            src, rows, target = x_buf.at[0, :, pl.ds(nz, REACH), :], pl.ds(2 * nz, REACH), slab_at(n_slab - 1)
        return remote(
            src, x_buf.at[slot, :, rows, :], x_ss.at[part, away], x_rs.at[part, slot], {"beam": beam_at(away), "slab": target}
        )

    order = sorted(range(n_beam), key=lambda away: abs(2 * away - n_beam))
    lines = [(part, away) for away in order for part in (0, 2)] + [(1, away) for away in order if away]

    def slab_copy(away, receiving):
        source = slab_at(away) if receiving else slab
        rows = pl.ds(pl.multiple_of(source * nz, nz), nz)
        slot = away if receiving else n_slab - away
        return remote(
            xl.at[:, pl.ds(nz, nz), :], la.at[:, rows, :], la_ss.at[away], la_rs.at[slot], {"slab": slab_at(away)}
        )

    for copy in small:
        copy.wait()
    sigma = [[cross[s, index[e]] * c1 for e in range(n_e)] for s in range(n_s)]
    lam_near = [lam[s] * c2 for s in range(n_s)]
    lam_before = [lam[s] * (c2 / c1) for s in range(n_s)]

    tile = BLOCK * nz

    def totals_of(value, block, dst):
        pair = split_pair(value.reshape(tile, ny))
        hl[block * tile : (block + 1) * tile] = pair
        dst[block : block + 1, :] = row_totals(pair)

    for chunk in range(CHUNKS):
        for z in range(nz):
            load(chunk, z).wait()
        for block in range(chunk * per_chunk, (chunk + 1) * per_chunk):
            rows = pl.ds(block * BLOCK, BLOCK)
            absorb = lam_near[0] * c_buf[0, rows]
            for s in range(1, n_s):
                absorb = absorb + lam_near[s] * c_buf[s, rows]
            totals_of(absorb, block, ra_send)
    pl.semaphore_wait(barrier, det + len(near))
    for away in range(1, n_det):

        @pl.when(det - away >= 0)
        def _():
            depth_copy(away).start()

    relay(relay_one)

    def first(block, depth):
        depth = list(depth)
        for part in range(BLOCK // 4):
            rows = pl.ds(block * BLOCK + part * 4, 4)
            c = [c_buf[s, rows] for s in range(n_s)]
            for e in range(n_e):
                value = sigma[0][e] * c[0]
                for s in range(1, n_s):
                    value = value + sigma[s][e] * c[s]
                em[e, rows] = value
                for x in range(4):
                    inc[e, block * BLOCK + part * 4 + x] = jnp.exp(depth[e])
                    depth[e] = depth[e] - value[x]
        return tuple(depth)

    depth = lax.fori_loop(0, blocks, first, (jnp.zeros((nz, ny), F32),) * n_e)
    for e in range(n_e):
        ud_send[e] = depth[e]
    for away in range(1, n_beam):
        beam_copy(away).start()
    pl.semaphore_wait(relay_one, 2)
    relay(relay_two)

    for away in range(1, n_det):

        @pl.when(det + away >= n_det)
        def _():
            ra_recv[away] = jnp.zeros_like(ra_send)

        @pl.when(det - away < 0)
        def _():
            rc_recv[away] = jnp.zeros_like(rc_send)

    deep = lax.broadcasted_iota(jnp.int32, (2 * ny, ny), 0) % ny
    wide = lax.broadcasted_iota(jnp.int32, (2 * ny, ny), 1)
    beyond = jnp.where(deep > wide, -1.0, 0.0).astype(BF16)
    nearer_side = jnp.where(deep < wide, 1.0, 0.0).astype(BF16)

    for block in range(blocks):
        path = jnp.dot(hl[block * tile : (block + 1) * tile], beyond, preferred_element_type=F32)
        escape = jnp.exp(path).reshape(BLOCK, nz, ny)
        rows = pl.ds(block * BLOCK, BLOCK)
        for e in range(n_e):
            light = inc[e, rows] * escape
            inc[e, rows] = light
            em[e, rows] = em[e, rows] * light

    slices = lax.broadcasted_iota(jnp.int32, wt.shape, 0) - nz
    full = jnp.zeros(wt.shape, F32)
    for j in range(fan):
        tap = weight[j : j + 1, :].astype(F32)
        full = full + jnp.where(offset[...] + j == slices, tap, 0.0)
    wt[...] = full
    wx[...] = wt[pl.ds(pl.multiple_of(slab * nz, nz), 3 * nz), :]
    whole = wt[nz : nz + n_slab * nz, :]
    padded = jnp.concatenate([whole, jnp.zeros((128 - n_slab * nz, n_k), F32)], axis=0)
    wk[...] = jnp.transpose(padded)
    own = wx[nz : 2 * nz, :]
    for shift in range(2 * REACH + 1):
        other = wx[nz - REACH + shift : 2 * nz - REACH + shift, :]
        band[shift] = jnp.broadcast_to(jnp.sum(own * other, axis=1, keepdims=True), (nz, ny))
    load_measured.wait()
    for e in range(n_e):
        wm[e] = jnp.dot(own, meas[e], precision=HIGHEST, preferred_element_type=F32)

    for away in range(1, n_beam):
        beam_copy(away).wait_recv()
    upstream = jnp.zeros((n_e, nz, ny), F32)
    for slot in range(1, n_beam):
        upstream = upstream + jnp.where(beam + slot >= n_beam, 1.0, 0.0) * ud_recv[slot]
    up_buf[...] = jnp.exp(upstream)

    for away in range(1, n_det):

        @pl.when(det + away < n_det)
        def _():
            depth_copy(away).wait_recv()

    downstream = ra_recv[1]
    for away in range(2, n_det):
        downstream = downstream + ra_recv[away]
    for r, piece in enumerate(spread(jnp.exp(-downstream))):
        dmp[r * BLOCK : (r + 1) * BLOCK] = piece.reshape(BLOCK, nz, ny)

    def third(block, sums):
        rows = pl.ds(block * BLOCK, BLOCK)
        damp = dmp[rows]
        return tuple(sums[e] + jnp.sum(em[e, rows] * damp, axis=0) for e in range(n_e))

    sums = lax.fori_loop(0, blocks, third, (jnp.zeros((nz, ny), F32),) * n_e)
    for e in range(n_e):
        x_buf[0, e, nz : 2 * nz] = sums[e] * up_buf[e]
    pl.semaphore_wait(relay_two, 2)
    for part, away in lines:
        line_copy(part, away).start()

    def fourth(count, after):
        block = blocks - 1 - count
        after = list(after)
        for x in range(BLOCK - 1, -1, -1):
            row = block * BLOCK + x
            damp = dmp[row]
            for e in range(n_e):
                fluor = em[e, row] * damp
                inc[e, row] = inc[e, row] * damp - after[e]
                em[e, row] = fluor
                after[e] = after[e] + fluor
        return tuple(after)

    lax.fori_loop(0, blocks, fourth, (jnp.zeros((nz, ny), F32),) * n_e)

    for part, away in lines:
        line_copy(part, away).wait_recv()
    middle = slice(nz - REACH, 2 * nz + REACH)
    extent = x_buf[0, :, middle]
    for slot in range(1, n_beam):
        extent = extent + x_buf[slot, :, middle]
    xl[:, middle] = extent
    further = jnp.zeros((n_e, nz, ny), F32)
    for slot in range(1, n_beam):
        further = further + jnp.where(beam + slot < n_beam, 1.0, 0.0) * x_buf[slot, :, nz : 2 * nz]
    back = []
    for e in range(n_e):
        value = band[0] * xl[e, nz - REACH : 2 * nz - REACH]
        for shift in range(1, 2 * REACH + 1):
            value = value + band[shift] * xl[e, nz - REACH + shift : 2 * nz - REACH + shift]
        back.append(value * (1.0 / 1.5) - wm[e])
    lit = [back[e] * up_buf[e] for e in range(n_e)]

    for block in range(blocks):
        rows = pl.ds(block * BLOCK, BLOCK)
        heavy = lit[0] * em[0, rows]
        for e in range(1, n_e):
            heavy = heavy + lit[e] * em[e, rows]
        totals_of(heavy, block, rc_send)
    for away in range(1, n_det):

        @pl.when(det + away < n_det)
        def _():
            column_copy(away).start()

    for away in range(1, n_slab):
        slab_copy(away, False).start()
    la[:, pl.ds(pl.multiple_of(slab * nz, nz), nz), :] = xl[:, nz : 2 * nz, :]
    shade = [back[e] * further[e] for e in range(n_e)]
    mix, less = [], []
    for s in range(n_s):
        pull = [cross[s, index[e]] for e in range(n_e)]
        mix.append([pull[e] * lit[e] for e in range(n_e)])
        value = pull[0] * shade[0]
        for e in range(1, n_e):
            value = value + pull[e] * shade[e]
        less.append(value)

    for block in range(blocks):
        before = jnp.dot(hl[block * tile : (block + 1) * tile], nearer_side, preferred_element_type=F32)
        dmp[block * BLOCK : (block + 1) * BLOCK] = before.reshape(BLOCK, nz, ny)

    def sixth(block, carry):
        for part in range(BLOCK // 4):
            rows = pl.ds(block * BLOCK + part * 4, 4)
            term = [inc[e, rows] for e in range(n_e)]
            for s in range(n_s):
                value = mix[s][0] * term[0]
                for e in range(1, n_e):
                    value = value + mix[s][e] * term[e]
                part_out[s, rows] = value - less[s] - lam_before[s] * dmp[rows]
        return carry

    lax.fori_loop(0, blocks, sixth, 0)

    for away in range(1, n_slab):
        slab_copy(away, True).wait_recv()
    share = n_k // (n_beam * n_slab)
    mine = pl.ds(pl.multiple_of((beam * n_slab + slab) * share, share), share)
    for e in range(n_e):
        signal = jnp.dot(wk[mine, 0 : n_slab * nz], la[e], precision=HIGHEST, preferred_element_type=F32)
        resid[e] = signal * (1.0 / 1.5) - meas[e, mine]

    for away in range(1, n_det):

        @pl.when(det - away >= 0)
        def _():
            remote(rc_send, rc_recv.at[away], rc_ss.at[away], rc_rs.at[away], {"det": lax.rem(det + away, n_det)}).wait_recv()

    nearer = rc_recv[1]
    for away in range(2, n_det):
        nearer = nearer + rc_recv[away]
    near_out[...] = nearer
    for s in range(n_s):
        lam_out[s] = jnp.full((nz, ny), lam_before[s], F32)

    for away in range(1, n_det):

        @pl.when(det - away >= 0)
        def _():
            depth_copy(away).wait_send()

        @pl.when(det + away < n_det)
        def _():
            column_copy(away).wait_send()

    for away in range(1, n_beam):
        beam_copy(away).wait_send()
    for part, away in lines:
        line_copy(part, away).wait_send()
    for away in range(1, n_slab):
        slab_copy(away, False).wait_send()


def finish(part, near, lam_before, resid_in, out, resid, buf, out_sem):
    n_s, nx, nz, ny = part.shape
    step = nx // STORES
    resid[...] = resid_in[...]
    pieces = spread(near[...])

    def store(chunk, z):
        rows = pl.ds(chunk * step, step)
        return pltpu.make_async_copy(buf.at[:, rows, z, :], out.at[:, z, rows, :], out_sem.at[chunk, z])

    for chunk in range(STORES):
        for block in range(chunk * step // BLOCK, (chunk + 1) * step // BLOCK):
            rows = slice(block * BLOCK, (block + 1) * BLOCK)
            shift = pieces[block].reshape(BLOCK, nz, ny)
            for s in range(n_s):
                buf[s, rows] = part[s, rows] - lam_before[s] * shift
        for z in range(nz):
            store(chunk, z).start()
    for chunk in range(STORES):
        for z in range(nz):
            store(chunk, z).wait()


def solution(mesh):
    sizes = (mesh.shape["beam"], mesh.shape["det"], mesh.shape["slab"])
    n_beam, n_det, n_slab = sizes

    def shards(concentration, cross_section, line_attenuation, energy_index, fan_offset, fan_weight, measured):
        n_s, nz, nx, ny = concentration.shape
        n_e, n_k = measured.shape[0], measured.shape[1]
        share = n_k // (n_beam * n_slab)
        volume = pltpu.VMEM((n_e, nx, nz, ny), F32)
        compact = (nx * nz // 128, 128)
        dma = pltpu.SemaphoreType.DMA
        scratch = [
            pltpu.SMEM(cross_section.shape, F32),
            pltpu.SMEM(line_attenuation.shape, F32),
            pltpu.SMEM(energy_index.shape, jnp.int32),
            pltpu.VMEM((1, n_k), jnp.int32),
            pltpu.VMEM((fan_weight.shape[1], n_k), jnp.int32),
            pltpu.VMEM((n_s, nx, nz, ny), F32),
            volume,
            volume,
            pltpu.VMEM((nx, nz, ny), F32),
            pltpu.VMEM((nx * nz, 2 * ny), BF16),
            pltpu.VMEM((n_e, n_k, ny), F32),
            pltpu.VMEM(((n_slab + 2) * nz, n_k), F32),
            pltpu.VMEM((3 * nz, n_k), F32),
            pltpu.VMEM((n_k, 128), F32),
            pltpu.VMEM((2 * REACH + 1, nz, ny), F32),
            pltpu.VMEM((n_e, nz, ny), F32),
            pltpu.VMEM((n_e, nz, ny), F32),
            pltpu.VMEM(compact, F32),
            pltpu.VMEM((n_det, *compact), F32),
            pltpu.VMEM((n_e, nz, ny), F32),
            pltpu.VMEM((n_beam, n_e, nz, ny), F32),
            pltpu.VMEM((n_beam, n_e, 3 * nz, ny), F32),
            pltpu.VMEM((n_e, 3 * nz, ny), F32),
            pltpu.VMEM((n_e, n_slab * nz, ny), F32),
            pltpu.VMEM(compact, F32),
            pltpu.VMEM((n_det, *compact), F32),
            dma((STORES, nz)),
            dma((5,)),
            dma,
            dma((n_det,)),
            dma((n_det,)),
            dma((n_beam,)),
            dma((n_beam,)),
            dma((3, n_beam)),
            dma((3, n_beam)),
            dma((n_slab,)),
            dma((n_slab,)),
            dma((n_det,)),
            dma((n_det,)),
            pltpu.SemaphoreType.REGULAR,
            pltpu.SemaphoreType.REGULAR,
        ]
        hbm = pl.BlockSpec(memory_space=pltpu.HBM)
        vmem = pl.BlockSpec(memory_space=pltpu.VMEM)
        share_shape = (n_e, share, ny)
        passed = pl.pallas_call(
            functools.partial(kernel, sizes),
            out_shape=(
                pltpu.VMEM((n_s, nx, nz, ny), F32),
                pltpu.VMEM(compact, F32),
                pltpu.VMEM((n_s, nz, ny), F32),
                pltpu.VMEM(share_shape, F32),
            ),
            in_specs=[hbm] * 7,
            out_specs=(vmem,) * 4,
            scratch_shapes=scratch,
            compiler_params=pltpu.CompilerParams(
                collective_id=0, has_side_effects=True, vmem_limit_bytes=28 * 2**20
            ),
        )(
            *(
                pltpu.with_memory_space_constraint(array, pltpu.HBM)
                for array in (
                    concentration,
                    cross_section,
                    line_attenuation,
                    energy_index,
                    fan_offset.reshape(1, n_k),
                    fan_weight.T,
                    measured,
                )
            )
        )
        return pl.pallas_call(
            finish,
            out_shape=(
                jax.ShapeDtypeStruct(concentration.shape, F32),
                jax.ShapeDtypeStruct(share_shape, F32),
            ),
            in_specs=[vmem] * 4,
            out_specs=(hbm, vmem),
            scratch_shapes=[pltpu.VMEM((n_s, nx, nz, ny), F32), dma((STORES, nz))],
            compiler_params=pltpu.CompilerParams(vmem_limit_bytes=16 * 2**20),
        )(*passed)

    in_specs = (P(None, "slab", "beam", "det"), P(), P(), P(), P(), P(), P(None, None, "det"))
    out_specs = (P(None, "slab", "beam", "det"), P(None, ("beam", "slab"), "det"))
    return jax.shard_map(shards, mesh=mesh, in_specs=in_specs, out_specs=out_specs, check_vma=False)
```

```python
import functools

import jax
import jax.numpy as jnp
from jax import lax
from jax.experimental import pallas as pl
from jax.experimental.pallas import tpu as pltpu
from jax.sharding import PartitionSpec as P

MESH = pl.DeviceIdType.MESH
F32 = jnp.float32
BF16 = jnp.bfloat16
HIGHEST = lax.Precision.HIGHEST
CHUNKS = 2
STORES = 4
BLOCK = 16
REACH = 3


def split_pair(value):
    high = value.astype(BF16)
    low = (value - high.astype(F32)).astype(BF16)
    return jnp.concatenate([high, low], axis=1)


def row_totals(pair):
    ones = jnp.ones((8, pair.shape[1]), BF16)
    total = lax.dot_general(ones, pair, (((1,), (1,)), ((), ())), preferred_element_type=F32)
    return total[0:1]


def spread(compact):
    rows = compact.shape[0]
    padded = jnp.concatenate([compact, jnp.zeros((128 - rows, 128), F32)], axis=0)
    turned = jnp.transpose(padded)
    return [jnp.broadcast_to(turned[:, r : r + 1], (128, 128)) for r in range(rows)]


def kernel(
    sizes, conc, cross_in, lam_in, index_in, offset_in, weight_in, measured, part_out, near_out, lam_out, resid,
    cross, lam, index, offset, weight, c_buf, em, inc, dmp, hl, meas, wt, wx, wk, band, wm, up_buf,
    ra_send, ra_recv, ud_send, ud_recv, x_buf, xl, la, rc_send, rc_recv,
    in_sem, small_sem, meas_sem, ra_ss, ra_rs, ud_ss, ud_rs, x_ss, x_rs, la_ss, la_rs, rc_ss, rc_rs, relays,
):
    n_beam, n_det, n_slab = sizes
    n_s, nz, nx, ny = conc.shape
    n_e = measured.shape[0]
    n_k = measured.shape[1]
    fan = weight_in.shape[0]
    c1 = 1.5 / (nx * n_beam)
    c2 = 1.5 / (ny * n_det)
    blocks = nx // BLOCK
    step = nx // CHUNKS
    per_chunk = blocks // CHUNKS
    beam, det, slab = lax.axis_index("beam"), lax.axis_index("det"), lax.axis_index("slab")

    def load(chunk, z):
        rows = pl.ds(chunk * step, step)
        return pltpu.make_async_copy(conc.at[:, z, rows, :], c_buf.at[:, rows, z, :], in_sem.at[chunk, z])

    pairs = ((cross_in, cross), (lam_in, lam), (index_in, index), (offset_in, offset), (weight_in, weight))
    small = [pltpu.make_async_copy(src, dst, small_sem.at[n]) for n, (src, dst) in enumerate(pairs)]
    for copy in small:
        copy.start()
    for chunk in range(CHUNKS):
        for z in range(nz):
            load(chunk, z).start()
    load_measured = pltpu.make_async_copy(measured, meas, meas_sem)
    load_measured.start()

    def beam_at(away):
        return lax.rem(beam + away, n_beam)

    def slab_at(away):
        return lax.rem(slab + away, n_slab)

    cores = 2
    deep_chips = n_beam // cores
    chips = deep_chips * n_slab
    chip, core = slab * deep_chips + beam // cores, lax.rem(beam, cores)

    def chip_at(away, core_at):
        there = lax.rem(chip + away + chips, chips)
        return {"beam": lax.rem(there, deep_chips) * cores + core_at, "slab": there // deep_chips}

    has = {-1: chip > 0, 1: chip < chips - 1}
    beside = jnp.where(has[-1], 1, 0) + jnp.where(has[1], 1, 0)
    barrier = pltpu.get_barrier_semaphore()
    for away in range(1, n_det):

        @pl.when(det + away < n_det)
        def _():
            pl.semaphore_signal(barrier, inc=1, device_id={"det": lax.rem(det + away, n_det)}, device_id_type=MESH)

    other_core = {"beam": beam + 1 - 2 * core}
    pl.semaphore_signal(barrier, inc=1, device_id=other_core, device_id_type=MESH)
    for away in (-1, 1):

        @pl.when(has[away])
        def _():
            for c in range(cores):
                pl.semaphore_signal(barrier, inc=1, device_id=chip_at(away, c), device_id_type=MESH)

    def tell(turn):
        for away in (-1, 1):

            @pl.when(has[away])
            def _():
                pl.semaphore_signal(relays.at[turn], inc=1, device_id=chip_at(away, core), device_id_type=MESH)

    def hear(turn):
        pl.semaphore_wait(relays.at[turn], beside)

    def remote(src, dst, send, recv, device):
        return pltpu.make_async_remote_copy(
            src_ref=src, dst_ref=dst, send_sem=send, recv_sem=recv, device_id=device, device_id_type=MESH
        )

    def depth_copy(away):
        return remote(ra_send, ra_recv.at[away], ra_ss.at[away], ra_rs.at[away], {"det": lax.rem(det - away + n_det, n_det)})

    def column_copy(away):
        return remote(rc_send, rc_recv.at[away], rc_ss.at[away], rc_rs.at[away], {"det": lax.rem(det + away, n_det)})

    def beam_copy(away):
        slot = n_beam - away
        return remote(ud_send, ud_recv.at[slot], ud_ss.at[away], ud_rs.at[slot], {"beam": beam_at(away)})

    def line_copy(part, away):
        slot = (n_beam - away) % n_beam
        if part == 1:
            src, rows, target = x_buf.at[0, :, pl.ds(nz, nz), :], pl.ds(nz, nz), slab
        elif part == 0:
            src, rows, target = x_buf.at[0, :, pl.ds(2 * nz - REACH, REACH), :], pl.ds(nz - REACH, REACH), slab_at(1)
        else:
            src, rows, target = x_buf.at[0, :, pl.ds(nz, REACH), :], pl.ds(2 * nz, REACH), slab_at(n_slab - 1)
        return remote(
            src, x_buf.at[slot, :, rows, :], x_ss.at[part, away], x_rs.at[part, slot], {"beam": beam_at(away), "slab": target}
        )

    order = sorted(range(n_beam), key=lambda away: abs(2 * away - n_beam))
    lines = [(part, away) for away in order for part in (0, 2)] + [(1, away) for away in order if away]

    def slab_copy(away, receiving):
        source = slab_at(away) if receiving else slab
        rows = pl.ds(pl.multiple_of(source * nz, nz), nz)
        slot = away if receiving else n_slab - away
        return remote(
            xl.at[:, pl.ds(nz, nz), :], la.at[:, rows, :], la_ss.at[away], la_rs.at[slot], {"slab": slab_at(away)}
        )

    for copy in small:
        copy.wait()
    sigma = [[cross[s, index[e]] * c1 for e in range(n_e)] for s in range(n_s)]
    lam_near = [lam[s] * c2 for s in range(n_s)]
    lam_before = [lam[s] * (c2 / c1) for s in range(n_s)]

    tile = BLOCK * nz

    def totals_of(value, block, dst):
        pair = split_pair(value.reshape(tile, ny))
        hl[block * tile : (block + 1) * tile] = pair
        dst[block : block + 1, :] = row_totals(pair)

    for chunk in range(CHUNKS):
        for z in range(nz):
            load(chunk, z).wait()
        for block in range(chunk * per_chunk, (chunk + 1) * per_chunk):
            rows = pl.ds(block * BLOCK, BLOCK)
            absorb = lam_near[0] * c_buf[0, rows]
            for s in range(1, n_s):
                absorb = absorb + lam_near[s] * c_buf[s, rows]
            totals_of(absorb, block, ra_send)
    pl.semaphore_wait(barrier, det + 1 + cores * beside)
    for away in range(1, n_det):

        @pl.when(det - away >= 0)
        def _():
            depth_copy(away).start()

    tell(0)

    def first(block, depth):
        depth = list(depth)
        for part in range(BLOCK // 4):
            rows = pl.ds(block * BLOCK + part * 4, 4)
            c = [c_buf[s, rows] for s in range(n_s)]
            for e in range(n_e):
                value = sigma[0][e] * c[0]
                for s in range(1, n_s):
                    value = value + sigma[s][e] * c[s]
                em[e, rows] = value
                for x in range(4):
                    inc[e, block * BLOCK + part * 4 + x] = jnp.exp(depth[e])
                    depth[e] = depth[e] - value[x]
        return tuple(depth)

    depth = lax.fori_loop(0, blocks, first, (jnp.zeros((nz, ny), F32),) * n_e)
    for e in range(n_e):
        ud_send[e] = depth[e]
    for away in range(1, n_beam):
        beam_copy(away).start()
    hear(0)
    tell(1)

    for away in range(1, n_det):

        @pl.when(det + away >= n_det)
        def _():
            ra_recv[away] = jnp.zeros_like(ra_send)

        @pl.when(det - away < 0)
        def _():
            rc_recv[away] = jnp.zeros_like(rc_send)

    no_halo = jnp.zeros((n_beam, n_e, REACH, ny), F32)

    @pl.when(slab == 0)
    def _():
        x_buf[:, :, nz - REACH : nz] = no_halo

    @pl.when(slab == n_slab - 1)
    def _():
        x_buf[:, :, 2 * nz : 2 * nz + REACH] = no_halo

    deep = lax.broadcasted_iota(jnp.int32, (2 * ny, ny), 0) % ny
    wide = lax.broadcasted_iota(jnp.int32, (2 * ny, ny), 1)
    beyond = jnp.where(deep > wide, -1.0, 0.0).astype(BF16)
    nearer_side = jnp.where(deep < wide, 1.0, 0.0).astype(BF16)

    for block in range(blocks):
        path = jnp.dot(hl[block * tile : (block + 1) * tile], beyond, preferred_element_type=F32)
        escape = jnp.exp(path).reshape(BLOCK, nz, ny)
        rows = pl.ds(block * BLOCK, BLOCK)
        for e in range(n_e):
            light = inc[e, rows] * escape
            inc[e, rows] = light
            em[e, rows] = em[e, rows] * light

    slices = lax.broadcasted_iota(jnp.int32, wt.shape, 0) - nz
    full = jnp.zeros(wt.shape, F32)
    for j in range(fan):
        tap = weight[j : j + 1, :].astype(F32)
        full = full + jnp.where(offset[...] + j == slices, tap, 0.0)
    wt[...] = full
    wx[...] = wt[pl.ds(pl.multiple_of(slab * nz, nz), 3 * nz), :]
    whole = wt[nz : nz + n_slab * nz, :]
    padded = jnp.concatenate([whole, jnp.zeros((128 - n_slab * nz, n_k), F32)], axis=0)
    wk[...] = jnp.transpose(padded)
    own = wx[nz : 2 * nz, :]
    for shift in range(2 * REACH + 1):
        other = wx[nz - REACH + shift : 2 * nz - REACH + shift, :]
        band[shift] = jnp.broadcast_to(jnp.sum(own * other, axis=1, keepdims=True), (nz, ny))
    load_measured.wait()
    for e in range(n_e):
        wm[e] = jnp.dot(own, meas[e], precision=HIGHEST, preferred_element_type=F32)

    hear(1)
    tell(2)
    for away in range(1, n_beam):
        beam_copy(away).wait_recv()
    upstream = jnp.zeros((n_e, nz, ny), F32)
    for slot in range(1, n_beam):
        upstream = upstream + jnp.where(beam + slot >= n_beam, 1.0, 0.0) * ud_recv[slot]
    up_buf[...] = jnp.exp(upstream)

    for away in range(1, n_det):

        @pl.when(det + away < n_det)
        def _():
            depth_copy(away).wait_recv()

    downstream = ra_recv[1]
    for away in range(2, n_det):
        downstream = downstream + ra_recv[away]
    for r, piece in enumerate(spread(jnp.exp(-downstream))):
        dmp[r * BLOCK : (r + 1) * BLOCK] = piece.reshape(BLOCK, nz, ny)

    def third(block, sums):
        rows = pl.ds(block * BLOCK, BLOCK)
        damp = dmp[rows]
        return tuple(sums[e] + jnp.sum(em[e, rows] * damp, axis=0) for e in range(n_e))

    sums = lax.fori_loop(0, blocks, third, (jnp.zeros((nz, ny), F32),) * n_e)
    for e in range(n_e):
        x_buf[0, e, nz : 2 * nz] = sums[e] * up_buf[e]
    hear(2)
    tell(3)
    send_if = {0: slab < n_slab - 1, 1: slab >= 0, 2: slab > 0}
    take_if = {0: slab > 0, 1: slab >= 0, 2: slab < n_slab - 1}
    for part, away in lines:

        @pl.when(send_if[part])
        def _():
            line_copy(part, away).start()


    def fourth(count, after):
        block = blocks - 1 - count
        after = list(after)
        for x in range(BLOCK - 1, -1, -1):
            row = block * BLOCK + x
            damp = dmp[row]
            for e in range(n_e):
                fluor = em[e, row] * damp
                inc[e, row] = inc[e, row] * damp - after[e]
                em[e, row] = fluor
                after[e] = after[e] + fluor
        return tuple(after)

    lax.fori_loop(0, blocks, fourth, (jnp.zeros((nz, ny), F32),) * n_e)

    hear(3)
    tell(4)
    for part, away in lines:

        @pl.when(take_if[part])
        def _():
            line_copy(part, away).wait_recv()

    middle = slice(nz - REACH, 2 * nz + REACH)
    extent = x_buf[0, :, middle]
    for slot in range(1, n_beam):
        extent = extent + x_buf[slot, :, middle]
    xl[:, middle] = extent
    further = jnp.zeros((n_e, nz, ny), F32)
    for slot in range(1, n_beam):
        further = further + jnp.where(beam + slot < n_beam, 1.0, 0.0) * x_buf[slot, :, nz : 2 * nz]
    back = []
    for e in range(n_e):
        value = band[0] * xl[e, nz - REACH : 2 * nz - REACH]
        for shift in range(1, 2 * REACH + 1):
            value = value + band[shift] * xl[e, nz - REACH + shift : 2 * nz - REACH + shift]
        back.append(value * (1.0 / 1.5) - wm[e])
    lit = [back[e] * up_buf[e] for e in range(n_e)]

    for block in range(blocks):
        rows = pl.ds(block * BLOCK, BLOCK)
        heavy = lit[0] * em[0, rows]
        for e in range(1, n_e):
            heavy = heavy + lit[e] * em[e, rows]
        totals_of(heavy, block, rc_send)
    for away in range(1, n_det):

        @pl.when(det + away < n_det)
        def _():
            column_copy(away).start()

    la[:, pl.ds(pl.multiple_of(slab * nz, nz), nz), :] = xl[:, nz : 2 * nz, :]
    shade = [back[e] * further[e] for e in range(n_e)]
    mix, less = [], []
    for s in range(n_s):
        pull = [cross[s, index[e]] for e in range(n_e)]
        mix.append([pull[e] * lit[e] for e in range(n_e)])
        value = pull[0] * shade[0]
        for e in range(1, n_e):
            value = value + pull[e] * shade[e]
        less.append(value)

    for block in range(blocks):
        before = jnp.dot(hl[block * tile : (block + 1) * tile], nearer_side, preferred_element_type=F32)
        dmp[block * BLOCK : (block + 1) * BLOCK] = before.reshape(BLOCK, nz, ny)

    def sixth(block, carry):
        for part in range(BLOCK // 4):
            rows = pl.ds(block * BLOCK + part * 4, 4)
            term = [inc[e, rows] for e in range(n_e)]
            for s in range(n_s):
                value = mix[s][0] * term[0]
                for e in range(1, n_e):
                    value = value + mix[s][e] * term[e]
                part_out[s, rows] = value - less[s] - lam_before[s] * dmp[rows]
        return carry

    lax.fori_loop(0, blocks, sixth, 0)

    def take_columns():
        for away in range(1, n_det):

            @pl.when(det - away >= 0)
            def _():
                remote(rc_send, rc_recv.at[away], rc_ss.at[away], rc_rs.at[away], {"det": lax.rem(det + away, n_det)}).wait_recv()

    hear(4)
    for away in range(1, n_slab):
        slab_copy(away, False).start()
    take_columns()
    for away in range(1, n_slab):
        slab_copy(away, True).wait_recv()
    share = n_k // (n_beam * n_slab)
    mine = pl.ds(pl.multiple_of((beam * n_slab + slab) * share, share), share)
    for e in range(n_e):
        signal = jnp.dot(wk[mine, 0 : n_slab * nz], la[e], precision=HIGHEST, preferred_element_type=F32)
        resid[e] = signal * (1.0 / 1.5) - meas[e, mine]

    nearer = rc_recv[1]
    for away in range(2, n_det):
        nearer = nearer + rc_recv[away]
    near_out[...] = nearer
    for s in range(n_s):
        lam_out[s] = jnp.full((nz, ny), lam_before[s], F32)

    for away in range(1, n_det):

        @pl.when(det - away >= 0)
        def _():
            depth_copy(away).wait_send()

        @pl.when(det + away < n_det)
        def _():
            column_copy(away).wait_send()

    for away in range(1, n_beam):
        beam_copy(away).wait_send()
    for part, away in lines:

        @pl.when(send_if[part])
        def _():
            line_copy(part, away).wait_send()

    for away in range(1, n_slab):
        slab_copy(away, False).wait_send()


def finish(part, near, lam_before, resid_in, out, resid, buf, out_sem):
    n_s, nx, nz, ny = part.shape
    step = nx // STORES
    resid[...] = resid_in[...]
    pieces = spread(near[...])

    def store(chunk, z):
        rows = pl.ds(chunk * step, step)
        return pltpu.make_async_copy(buf.at[:, rows, z, :], out.at[:, z, rows, :], out_sem.at[chunk, z])

    for chunk in range(STORES):
        for block in range(chunk * step // BLOCK, (chunk + 1) * step // BLOCK):
            rows = slice(block * BLOCK, (block + 1) * BLOCK)
            shift = pieces[block].reshape(BLOCK, nz, ny)
            for s in range(n_s):
                buf[s, rows] = part[s, rows] - lam_before[s] * shift
        for z in range(nz):
            store(chunk, z).start()
    for chunk in range(STORES):
        for z in range(nz):
            store(chunk, z).wait()


def solution(mesh):
    sizes = (mesh.shape["beam"], mesh.shape["det"], mesh.shape["slab"])
    n_beam, n_det, n_slab = sizes

    def shards(concentration, cross_section, line_attenuation, energy_index, fan_offset, fan_weight, measured):
        n_s, nz, nx, ny = concentration.shape
        n_e, n_k = measured.shape[0], measured.shape[1]
        share = n_k // (n_beam * n_slab)
        volume = pltpu.VMEM((n_e, nx, nz, ny), F32)
        compact = (nx * nz // 128, 128)
        dma = pltpu.SemaphoreType.DMA
        scratch = [
            pltpu.SMEM(cross_section.shape, F32),
            pltpu.SMEM(line_attenuation.shape, F32),
            pltpu.SMEM(energy_index.shape, jnp.int32),
            pltpu.VMEM((1, n_k), jnp.int32),
            pltpu.VMEM((fan_weight.shape[1], n_k), jnp.int32),
            pltpu.VMEM((n_s, nx, nz, ny), F32),
            volume,
            volume,
            pltpu.VMEM((nx, nz, ny), F32),
            pltpu.VMEM((nx * nz, 2 * ny), BF16),
            pltpu.VMEM((n_e, n_k, ny), F32),
            pltpu.VMEM(((n_slab + 2) * nz, n_k), F32),
            pltpu.VMEM((3 * nz, n_k), F32),
            pltpu.VMEM((n_k, 128), F32),
            pltpu.VMEM((2 * REACH + 1, nz, ny), F32),
            pltpu.VMEM((n_e, nz, ny), F32),
            pltpu.VMEM((n_e, nz, ny), F32),
            pltpu.VMEM(compact, F32),
            pltpu.VMEM((n_det, *compact), F32),
            pltpu.VMEM((n_e, nz, ny), F32),
            pltpu.VMEM((n_beam, n_e, nz, ny), F32),
            pltpu.VMEM((n_beam, n_e, 3 * nz, ny), F32),
            pltpu.VMEM((n_e, 3 * nz, ny), F32),
            pltpu.VMEM((n_e, n_slab * nz, ny), F32),
            pltpu.VMEM(compact, F32),
            pltpu.VMEM((n_det, *compact), F32),
            dma((STORES, nz)),
            dma((5,)),
            dma,
            dma((n_det,)),
            dma((n_det,)),
            dma((n_beam,)),
            dma((n_beam,)),
            dma((3, n_beam)),
            dma((3, n_beam)),
            dma((n_slab,)),
            dma((n_slab,)),
            dma((n_det,)),
            dma((n_det,)),
            pltpu.SemaphoreType.REGULAR((5,)),
        ]
        hbm = pl.BlockSpec(memory_space=pltpu.HBM)
        vmem = pl.BlockSpec(memory_space=pltpu.VMEM)
        share_shape = (n_e, share, ny)
        passed = pl.pallas_call(
            functools.partial(kernel, sizes),
            out_shape=(
                pltpu.VMEM((n_s, nx, nz, ny), F32),
                pltpu.VMEM(compact, F32),
                pltpu.VMEM((n_s, nz, ny), F32),
                pltpu.VMEM(share_shape, F32),
            ),
            in_specs=[hbm] * 7,
            out_specs=(vmem,) * 4,
            scratch_shapes=scratch,
            compiler_params=pltpu.CompilerParams(
                collective_id=0, has_side_effects=True, vmem_limit_bytes=28 * 2**20
            ),
        )(
            *(
                pltpu.with_memory_space_constraint(array, pltpu.HBM)
                for array in (
                    concentration,
                    cross_section,
                    line_attenuation,
                    energy_index,
                    fan_offset.reshape(1, n_k),
                    fan_weight.T,
                    measured,
                )
            )
        )
        return pl.pallas_call(
            finish,
            out_shape=(
                jax.ShapeDtypeStruct(concentration.shape, F32),
                jax.ShapeDtypeStruct(share_shape, F32),
            ),
            in_specs=[vmem] * 4,
            out_specs=(hbm, vmem),
            scratch_shapes=[pltpu.VMEM((n_s, nx, nz, ny), F32), dma((STORES, nz))],
            compiler_params=pltpu.CompilerParams(vmem_limit_bytes=16 * 2**20),
        )(*passed)

    in_specs = (P(None, "slab", "beam", "det"), P(), P(), P(), P(), P(), P(None, None, "det"))
    out_specs = (P(None, "slab", "beam", "det"), P(None, ("beam", "slab"), "det"))
    return jax.shard_map(shards, mesh=mesh, in_specs=in_specs, out_specs=out_specs, check_vma=False)
```

```python
import functools

import jax
import jax.numpy as jnp
from jax import lax
from jax.experimental import pallas as pl
from jax.experimental.pallas import tpu as pltpu
from jax.sharding import PartitionSpec as P

MESH = pl.DeviceIdType.MESH
F32 = jnp.float32
BF16 = jnp.bfloat16
HIGHEST = lax.Precision.HIGHEST
CHUNKS = 2
STORES = 4
BLOCK = 16
REACH = 3


def split_pair(value):
    high = value.astype(BF16)
    low = (value - high.astype(F32)).astype(BF16)
    return jnp.concatenate([high, low], axis=1)


def row_totals(pair):
    ones = jnp.ones((8, pair.shape[1]), BF16)
    total = lax.dot_general(ones, pair, (((1,), (1,)), ((), ())), preferred_element_type=F32)
    return total[0:1]


def spread(compact):
    rows = compact.shape[0]
    padded = jnp.concatenate([compact, jnp.zeros((128 - rows, 128), F32)], axis=0)
    turned = jnp.transpose(padded)
    return [jnp.broadcast_to(turned[:, r : r + 1], (128, 128)) for r in range(rows)]


def kernel(
    sizes, conc, cross_in, lam_in, index_in, offset_in, weight_in, measured, part_out, near_out, lam_out, resid,
    cross, lam, index, offset, weight, c_buf, em, inc, dmp, hl, meas, wt, wx, wk, band, wm, up_buf,
    ra_send, ra_recv, ud_send, ud_recv, x_buf, xl, la, rc_send, rc_recv,
    in_sem, small_sem, meas_sem, ra_ss, ra_rs, ud_ss, ud_rs, x_ss, x_rs, la_ss, la_rs, rc_ss, rc_rs, relays,
):
    n_beam, n_det, n_slab = sizes
    n_s, nz, nx, ny = conc.shape
    n_e = measured.shape[0]
    n_k = measured.shape[1]
    fan = weight_in.shape[0]
    c1 = 1.5 / (nx * n_beam)
    c2 = 1.5 / (ny * n_det)
    blocks = nx // BLOCK
    step = nx // CHUNKS
    per_chunk = blocks // CHUNKS
    beam, det, slab = lax.axis_index("beam"), lax.axis_index("det"), lax.axis_index("slab")

    def load(chunk, z):
        rows = pl.ds(chunk * step, step)
        return pltpu.make_async_copy(conc.at[:, z, rows, :], c_buf.at[:, rows, z, :], in_sem.at[chunk, z])

    pairs = ((cross_in, cross), (lam_in, lam), (index_in, index), (offset_in, offset), (weight_in, weight))
    small = [pltpu.make_async_copy(src, dst, small_sem.at[n]) for n, (src, dst) in enumerate(pairs)]
    for copy in small:
        copy.start()
    for chunk in range(CHUNKS):
        for z in range(nz):
            load(chunk, z).start()
    load_measured = pltpu.make_async_copy(measured, meas, meas_sem)
    load_measured.start()

    def beam_at(away):
        return lax.rem(beam + away, n_beam)

    def slab_at(away):
        return lax.rem(slab + away, n_slab)

    cores = 2
    deep_chips = n_beam // cores
    chips = deep_chips * n_slab
    chip, core = slab * deep_chips + beam // cores, lax.rem(beam, cores)

    def chip_at(away, core_at):
        there = lax.rem(chip + away + chips, chips)
        return {"beam": lax.rem(there, deep_chips) * cores + core_at, "slab": there // deep_chips}

    has = {-1: chip > 0, 1: chip < chips - 1}
    beside = jnp.where(has[-1], 1, 0) + jnp.where(has[1], 1, 0)
    barrier = pltpu.get_barrier_semaphore()
    for away in range(1, n_det):

        @pl.when(det + away < n_det)
        def _():
            pl.semaphore_signal(barrier, inc=1, device_id={"det": lax.rem(det + away, n_det)}, device_id_type=MESH)

    other_core = {"beam": beam + 1 - 2 * core}
    pl.semaphore_signal(barrier, inc=1, device_id=other_core, device_id_type=MESH)
    for away in (-1, 1):

        @pl.when(has[away])
        def _():
            for c in range(cores):
                pl.semaphore_signal(barrier, inc=1, device_id=chip_at(away, c), device_id_type=MESH)

    def tell(turn):
        for away in (-1, 1):

            @pl.when(has[away])
            def _():
                pl.semaphore_signal(relays.at[turn], inc=1, device_id=chip_at(away, core), device_id_type=MESH)

    def hear(turn):
        pl.semaphore_wait(relays.at[turn], beside)

    def remote(src, dst, send, recv, device):
        return pltpu.make_async_remote_copy(
            src_ref=src, dst_ref=dst, send_sem=send, recv_sem=recv, device_id=device, device_id_type=MESH
        )

    def depth_copy(away):
        return remote(ra_send, ra_recv.at[away], ra_ss.at[away], ra_rs.at[away], {"det": lax.rem(det - away + n_det, n_det)})

    def column_copy(away):
        return remote(rc_send, rc_recv.at[away], rc_ss.at[away], rc_rs.at[away], {"det": lax.rem(det + away, n_det)})

    def beam_copy(away):
        slot = n_beam - away
        return remote(ud_send, ud_recv.at[slot], ud_ss.at[away], ud_rs.at[slot], {"beam": beam_at(away)})

    def line_copy(part, away):
        slot = (n_beam - away) % n_beam
        if part == 1:
            src, rows, target = x_buf.at[0, :, pl.ds(nz, nz), :], pl.ds(nz, nz), slab
        elif part == 0:
            src, rows, target = x_buf.at[0, :, pl.ds(2 * nz - REACH, REACH), :], pl.ds(nz - REACH, REACH), slab_at(1)
        else:
            src, rows, target = x_buf.at[0, :, pl.ds(nz, REACH), :], pl.ds(2 * nz, REACH), slab_at(n_slab - 1)
        return remote(
            src, x_buf.at[slot, :, rows, :], x_ss.at[part, away], x_rs.at[part, slot], {"beam": beam_at(away), "slab": target}
        )

    order = sorted(range(n_beam), key=lambda away: abs(2 * away - n_beam))
    lines = [(part, away) for away in order for part in (0, 2)] + [(1, away) for away in order if away]

    def slab_copy(away, receiving):
        source = slab_at(away) if receiving else slab
        rows = pl.ds(pl.multiple_of(source * nz, nz), nz)
        slot = away if receiving else n_slab - away
        return remote(
            xl.at[:, pl.ds(nz, nz), :], la.at[:, rows, :], la_ss.at[away], la_rs.at[slot], {"slab": slab_at(away)}
        )

    for copy in small:
        copy.wait()
    sigma = [[cross[s, index[e]] * c1 for e in range(n_e)] for s in range(n_s)]
    lam_near = [lam[s] * c2 for s in range(n_s)]
    lam_before = [lam[s] * (c2 / c1) for s in range(n_s)]

    tile = BLOCK * nz

    def totals_of(value, block, dst):
        pair = split_pair(value.reshape(tile, ny))
        hl[block * tile : (block + 1) * tile] = pair
        dst[block : block + 1, :] = row_totals(pair)

    for chunk in range(CHUNKS):
        for z in range(nz):
            load(chunk, z).wait()
        for block in range(chunk * per_chunk, (chunk + 1) * per_chunk):
            rows = pl.ds(block * BLOCK, BLOCK)
            absorb = lam_near[0] * c_buf[0, rows]
            for s in range(1, n_s):
                absorb = absorb + lam_near[s] * c_buf[s, rows]
            totals_of(absorb, block, ra_send)
    pl.semaphore_wait(barrier, det + 1 + cores * beside)
    for away in range(1, n_det):

        @pl.when(det - away >= 0)
        def _():
            depth_copy(away).start()

    tell(0)

    def first(block, depth):
        depth = list(depth)
        for part in range(BLOCK // 4):
            rows = pl.ds(block * BLOCK + part * 4, 4)
            c = [c_buf[s, rows] for s in range(n_s)]
            for e in range(n_e):
                value = sigma[0][e] * c[0]
                for s in range(1, n_s):
                    value = value + sigma[s][e] * c[s]
                em[e, rows] = value
                for x in range(4):
                    inc[e, block * BLOCK + part * 4 + x] = jnp.exp(depth[e])
                    depth[e] = depth[e] - value[x]
        return tuple(depth)

    depth = lax.fori_loop(0, blocks, first, (jnp.zeros((nz, ny), F32),) * n_e)
    for e in range(n_e):
        ud_send[e] = depth[e]
    for away in range(1, n_beam):
        beam_copy(away).start()
    hear(0)
    tell(1)

    for away in range(1, n_det):

        @pl.when(det + away >= n_det)
        def _():
            ra_recv[away] = jnp.zeros_like(ra_send)

        @pl.when(det - away < 0)
        def _():
            rc_recv[away] = jnp.zeros_like(rc_send)

    no_halo = jnp.zeros((n_beam, n_e, REACH, ny), F32)

    @pl.when(slab == 0)
    def _():
        x_buf[:, :, nz - REACH : nz] = no_halo

    @pl.when(slab == n_slab - 1)
    def _():
        x_buf[:, :, 2 * nz : 2 * nz + REACH] = no_halo

    deep = lax.broadcasted_iota(jnp.int32, (2 * ny, ny), 0) % ny
    wide = lax.broadcasted_iota(jnp.int32, (2 * ny, ny), 1)
    beyond = jnp.where(deep > wide, -1.0, 0.0).astype(BF16)
    nearer_side = jnp.where(deep < wide, 1.0, 0.0).astype(BF16)

    for block in range(blocks):
        path = jnp.dot(hl[block * tile : (block + 1) * tile], beyond, preferred_element_type=F32)
        escape = jnp.exp(path).reshape(BLOCK, nz, ny)
        rows = pl.ds(block * BLOCK, BLOCK)
        for e in range(n_e):
            light = inc[e, rows] * escape
            inc[e, rows] = light
            em[e, rows] = em[e, rows] * light

    slices = lax.broadcasted_iota(jnp.int32, wt.shape, 0) - nz
    full = jnp.zeros(wt.shape, F32)
    for j in range(fan):
        tap = weight[j : j + 1, :].astype(F32)
        full = full + jnp.where(offset[...] + j == slices, tap, 0.0)
    wt[...] = full
    wx[...] = wt[pl.ds(pl.multiple_of(slab * nz, nz), 3 * nz), :]
    whole = wt[nz : nz + n_slab * nz, :]
    padded = jnp.concatenate([whole, jnp.zeros((128 - n_slab * nz, n_k), F32)], axis=0)
    wk[...] = jnp.transpose(padded)
    own = wx[nz : 2 * nz, :]
    for shift in range(2 * REACH + 1):
        other = wx[nz - REACH + shift : 2 * nz - REACH + shift, :]
        band[shift] = jnp.broadcast_to(jnp.sum(own * other, axis=1, keepdims=True), (nz, ny))
    load_measured.wait()
    for e in range(n_e):
        wm[e] = jnp.dot(own, meas[e], precision=HIGHEST, preferred_element_type=F32)

    hear(1)
    tell(2)
    for away in range(1, n_beam):
        beam_copy(away).wait_recv()
    upstream = jnp.zeros((n_e, nz, ny), F32)
    for slot in range(1, n_beam):
        upstream = upstream + jnp.where(beam + slot >= n_beam, 1.0, 0.0) * ud_recv[slot]
    up_buf[...] = jnp.exp(upstream)

    for away in range(1, n_det):

        @pl.when(det + away < n_det)
        def _():
            depth_copy(away).wait_recv()

    downstream = ra_recv[1]
    for away in range(2, n_det):
        downstream = downstream + ra_recv[away]
    for r, piece in enumerate(spread(jnp.exp(-downstream))):
        dmp[r * BLOCK : (r + 1) * BLOCK] = piece.reshape(BLOCK, nz, ny)

    def third(block, sums):
        rows = pl.ds(block * BLOCK, BLOCK)
        damp = dmp[rows]
        return tuple(sums[e] + jnp.sum(em[e, rows] * damp, axis=0) for e in range(n_e))

    sums = lax.fori_loop(0, blocks, third, (jnp.zeros((nz, ny), F32),) * n_e)
    for e in range(n_e):
        x_buf[0, e, nz : 2 * nz] = sums[e] * up_buf[e]
    send_if = {0: slab < n_slab - 1, 1: slab >= 0, 2: slab > 0}
    take_if = {0: slab > 0, 1: slab >= 0, 2: slab < n_slab - 1}
    for part, away in lines:

        @pl.when(send_if[part])
        def _():
            line_copy(part, away).start()

    hear(2)
    tell(3)

    def fourth(count, after):
        block = blocks - 1 - count
        after = list(after)
        for x in range(BLOCK - 1, -1, -1):
            row = block * BLOCK + x
            damp = dmp[row]
            for e in range(n_e):
                fluor = em[e, row] * damp
                inc[e, row] = inc[e, row] * damp - after[e]
                em[e, row] = fluor
                after[e] = after[e] + fluor
        return tuple(after)

    lax.fori_loop(0, blocks, fourth, (jnp.zeros((nz, ny), F32),) * n_e)

    hear(3)
    tell(4)
    for part, away in lines:

        @pl.when(take_if[part])
        def _():
            line_copy(part, away).wait_recv()

    middle = slice(nz - REACH, 2 * nz + REACH)
    extent = x_buf[0, :, middle]
    for slot in range(1, n_beam):
        extent = extent + x_buf[slot, :, middle]
    xl[:, middle] = extent
    further = jnp.zeros((n_e, nz, ny), F32)
    for slot in range(1, n_beam):
        further = further + jnp.where(beam + slot < n_beam, 1.0, 0.0) * x_buf[slot, :, nz : 2 * nz]
    back = []
    for e in range(n_e):
        value = band[0] * xl[e, nz - REACH : 2 * nz - REACH]
        for shift in range(1, 2 * REACH + 1):
            value = value + band[shift] * xl[e, nz - REACH + shift : 2 * nz - REACH + shift]
        back.append(value * (1.0 / 1.5) - wm[e])
    lit = [back[e] * up_buf[e] for e in range(n_e)]

    for block in range(blocks):
        rows = pl.ds(block * BLOCK, BLOCK)
        heavy = lit[0] * em[0, rows]
        for e in range(1, n_e):
            heavy = heavy + lit[e] * em[e, rows]
        totals_of(heavy, block, rc_send)
    for away in range(1, n_det):

        @pl.when(det + away < n_det)
        def _():
            column_copy(away).start()

    hear(4)
    for away in range(1, n_slab):
        slab_copy(away, False).start()
    la[:, pl.ds(pl.multiple_of(slab * nz, nz), nz), :] = xl[:, nz : 2 * nz, :]
    shade = [back[e] * further[e] for e in range(n_e)]
    mix, less = [], []
    for s in range(n_s):
        pull = [cross[s, index[e]] for e in range(n_e)]
        mix.append([pull[e] * lit[e] for e in range(n_e)])
        value = pull[0] * shade[0]
        for e in range(1, n_e):
            value = value + pull[e] * shade[e]
        less.append(value)

    for block in range(blocks):
        before = jnp.dot(hl[block * tile : (block + 1) * tile], nearer_side, preferred_element_type=F32)
        dmp[block * BLOCK : (block + 1) * BLOCK] = before.reshape(BLOCK, nz, ny)

    def sixth(block, carry):
        for part in range(BLOCK // 4):
            rows = pl.ds(block * BLOCK + part * 4, 4)
            term = [inc[e, rows] for e in range(n_e)]
            for s in range(n_s):
                value = mix[s][0] * term[0]
                for e in range(1, n_e):
                    value = value + mix[s][e] * term[e]
                part_out[s, rows] = value - less[s] - lam_before[s] * dmp[rows]
        return carry

    lax.fori_loop(0, blocks, sixth, 0)

    def take_columns():
        for away in range(1, n_det):

            @pl.when(det - away >= 0)
            def _():
                remote(rc_send, rc_recv.at[away], rc_ss.at[away], rc_rs.at[away], {"det": lax.rem(det + away, n_det)}).wait_recv()

    take_columns()
    for away in range(1, n_slab):
        slab_copy(away, True).wait_recv()
    share = n_k // (n_beam * n_slab)
    mine = pl.ds(pl.multiple_of((beam * n_slab + slab) * share, share), share)
    for e in range(n_e):
        signal = jnp.dot(wk[mine, 0 : n_slab * nz], la[e], precision=HIGHEST, preferred_element_type=F32)
        resid[e] = signal * (1.0 / 1.5) - meas[e, mine]

    nearer = rc_recv[1]
    for away in range(2, n_det):
        nearer = nearer + rc_recv[away]
    near_out[...] = nearer
    for s in range(n_s):
        lam_out[s] = jnp.full((nz, ny), lam_before[s], F32)

    for away in range(1, n_det):

        @pl.when(det - away >= 0)
        def _():
            depth_copy(away).wait_send()

        @pl.when(det + away < n_det)
        def _():
            column_copy(away).wait_send()

    for away in range(1, n_beam):
        beam_copy(away).wait_send()
    for part, away in lines:

        @pl.when(send_if[part])
        def _():
            line_copy(part, away).wait_send()

    for away in range(1, n_slab):
        slab_copy(away, False).wait_send()


def finish(part, near, lam_before, resid_in, out, resid, buf, out_sem):
    n_s, nx, nz, ny = part.shape
    step = nx // STORES
    resid[...] = resid_in[...]
    pieces = spread(near[...])

    def store(chunk, z):
        rows = pl.ds(chunk * step, step)
        return pltpu.make_async_copy(buf.at[:, rows, z, :], out.at[:, z, rows, :], out_sem.at[chunk, z])

    for chunk in range(STORES):
        for block in range(chunk * step // BLOCK, (chunk + 1) * step // BLOCK):
            rows = slice(block * BLOCK, (block + 1) * BLOCK)
            shift = pieces[block].reshape(BLOCK, nz, ny)
            for s in range(n_s):
                buf[s, rows] = part[s, rows] - lam_before[s] * shift
        for z in range(nz):
            store(chunk, z).start()
    for chunk in range(STORES):
        for z in range(nz):
            store(chunk, z).wait()


def solution(mesh):
    sizes = (mesh.shape["beam"], mesh.shape["det"], mesh.shape["slab"])
    n_beam, n_det, n_slab = sizes

    def shards(concentration, cross_section, line_attenuation, energy_index, fan_offset, fan_weight, measured):
        n_s, nz, nx, ny = concentration.shape
        n_e, n_k = measured.shape[0], measured.shape[1]
        share = n_k // (n_beam * n_slab)
        volume = pltpu.VMEM((n_e, nx, nz, ny), F32)
        compact = (nx * nz // 128, 128)
        dma = pltpu.SemaphoreType.DMA
        scratch = [
            pltpu.SMEM(cross_section.shape, F32),
            pltpu.SMEM(line_attenuation.shape, F32),
            pltpu.SMEM(energy_index.shape, jnp.int32),
            pltpu.VMEM((1, n_k), jnp.int32),
            pltpu.VMEM((fan_weight.shape[1], n_k), jnp.int32),
            pltpu.VMEM((n_s, nx, nz, ny), F32),
            volume,
            volume,
            pltpu.VMEM((nx, nz, ny), F32),
            pltpu.VMEM((nx * nz, 2 * ny), BF16),
            pltpu.VMEM((n_e, n_k, ny), F32),
            pltpu.VMEM(((n_slab + 2) * nz, n_k), F32),
            pltpu.VMEM((3 * nz, n_k), F32),
            pltpu.VMEM((n_k, 128), F32),
            pltpu.VMEM((2 * REACH + 1, nz, ny), F32),
            pltpu.VMEM((n_e, nz, ny), F32),
            pltpu.VMEM((n_e, nz, ny), F32),
            pltpu.VMEM(compact, F32),
            pltpu.VMEM((n_det, *compact), F32),
            pltpu.VMEM((n_e, nz, ny), F32),
            pltpu.VMEM((n_beam, n_e, nz, ny), F32),
            pltpu.VMEM((n_beam, n_e, 3 * nz, ny), F32),
            pltpu.VMEM((n_e, 3 * nz, ny), F32),
            pltpu.VMEM((n_e, n_slab * nz, ny), F32),
            pltpu.VMEM(compact, F32),
            pltpu.VMEM((n_det, *compact), F32),
            dma((STORES, nz)),
            dma((5,)),
            dma,
            dma((n_det,)),
            dma((n_det,)),
            dma((n_beam,)),
            dma((n_beam,)),
            dma((3, n_beam)),
            dma((3, n_beam)),
            dma((n_slab,)),
            dma((n_slab,)),
            dma((n_det,)),
            dma((n_det,)),
            pltpu.SemaphoreType.REGULAR((5,)),
        ]
        hbm = pl.BlockSpec(memory_space=pltpu.HBM)
        vmem = pl.BlockSpec(memory_space=pltpu.VMEM)
        share_shape = (n_e, share, ny)
        passed = pl.pallas_call(
            functools.partial(kernel, sizes),
            out_shape=(
                pltpu.VMEM((n_s, nx, nz, ny), F32),
                pltpu.VMEM(compact, F32),
                pltpu.VMEM((n_s, nz, ny), F32),
                pltpu.VMEM(share_shape, F32),
            ),
            in_specs=[hbm] * 7,
            out_specs=(vmem,) * 4,
            scratch_shapes=scratch,
            compiler_params=pltpu.CompilerParams(
                collective_id=0, has_side_effects=True, vmem_limit_bytes=28 * 2**20
            ),
        )(
            *(
                pltpu.with_memory_space_constraint(array, pltpu.HBM)
                for array in (
                    concentration,
                    cross_section,
                    line_attenuation,
                    energy_index,
                    fan_offset.reshape(1, n_k),
                    fan_weight.T,
                    measured,
                )
            )
        )
        return pl.pallas_call(
            finish,
            out_shape=(
                jax.ShapeDtypeStruct(concentration.shape, F32),
                jax.ShapeDtypeStruct(share_shape, F32),
            ),
            in_specs=[vmem] * 4,
            out_specs=(hbm, vmem),
            scratch_shapes=[pltpu.VMEM((n_s, nx, nz, ny), F32), dma((STORES, nz))],
            compiler_params=pltpu.CompilerParams(vmem_limit_bytes=16 * 2**20),
        )(*passed)

    in_specs = (P(None, "slab", "beam", "det"), P(), P(), P(), P(), P(), P(None, None, "det"))
    out_specs = (P(None, "slab", "beam", "det"), P(None, ("beam", "slab"), "det"))
    return jax.shard_map(shards, mesh=mesh, in_specs=in_specs, out_specs=out_specs, check_vma=False)
```

```python
import functools

import jax
import jax.numpy as jnp
from jax import lax
from jax.experimental import pallas as pl
from jax.experimental.pallas import tpu as pltpu
from jax.sharding import PartitionSpec as P

MESH = pl.DeviceIdType.MESH
F32 = jnp.float32
BF16 = jnp.bfloat16
HIGHEST = lax.Precision.HIGHEST
CHUNKS = 2
STORES = 4
BLOCK = 16
REACH = 3


def split_pair(value):
    high = value.astype(BF16)
    low = (value - high.astype(F32)).astype(BF16)
    return jnp.concatenate([high, low], axis=1)


def row_totals(pair):
    ones = jnp.ones((8, pair.shape[1]), BF16)
    total = lax.dot_general(ones, pair, (((1,), (1,)), ((), ())), preferred_element_type=F32)
    return total[0:1]


def spread(compact):
    rows = compact.shape[0]
    padded = jnp.concatenate([compact, jnp.zeros((128 - rows, 128), F32)], axis=0)
    turned = jnp.transpose(padded)
    return [jnp.broadcast_to(turned[:, r : r + 1], (128, 128)) for r in range(rows)]


def kernel(
    sizes, conc, cross_in, lam_in, index_in, offset_in, weight_in, measured, part_out, near_out, lam_out, resid,
    cross, lam, index, offset, weight, c_buf, em, inc, dmp, hl, meas, wt, wx, wk, band, wm, up_buf,
    ra_send, ra_recv, ud_send, ud_recv, x_buf, xl, la, rc_send, rc_recv,
    in_sem, small_sem, meas_sem, ra_ss, ra_rs, ud_ss, ud_rs, x_ss, x_rs, la_ss, la_rs, rc_ss, rc_rs, relays,
):
    n_beam, n_det, n_slab = sizes
    n_s, nz, nx, ny = conc.shape
    n_e = measured.shape[0]
    n_k = measured.shape[1]
    fan = weight_in.shape[0]
    c1 = 1.5 / (nx * n_beam)
    c2 = 1.5 / (ny * n_det)
    blocks = nx // BLOCK
    step = nx // CHUNKS
    per_chunk = blocks // CHUNKS
    beam, det, slab = lax.axis_index("beam"), lax.axis_index("det"), lax.axis_index("slab")

    def load(chunk, z):
        rows = pl.ds(chunk * step, step)
        return pltpu.make_async_copy(conc.at[:, z, rows, :], c_buf.at[:, rows, z, :], in_sem.at[chunk, z])

    pairs = ((cross_in, cross), (lam_in, lam), (index_in, index), (offset_in, offset), (weight_in, weight))
    small = [pltpu.make_async_copy(src, dst, small_sem.at[n]) for n, (src, dst) in enumerate(pairs)]
    for copy in small:
        copy.start()
    for chunk in range(CHUNKS):
        for z in range(nz):
            load(chunk, z).start()
    load_measured = pltpu.make_async_copy(measured, meas, meas_sem)
    load_measured.start()

    def beam_at(away):
        return lax.rem(beam + away, n_beam)

    def slab_at(away):
        return lax.rem(slab + away, n_slab)

    cores = 2
    deep_chips = n_beam // cores
    chips = deep_chips * n_slab
    chip, core = slab * deep_chips + beam // cores, lax.rem(beam, cores)

    def chip_at(away, core_at):
        there = lax.rem(chip + away + chips, chips)
        return {"beam": lax.rem(there, deep_chips) * cores + core_at, "slab": there // deep_chips}

    has = {-1: chip > 0, 1: chip < chips - 1}
    beside = jnp.where(has[-1], 1, 0) + jnp.where(has[1], 1, 0)
    barrier = pltpu.get_barrier_semaphore()
    for away in range(1, n_det):

        @pl.when(det + away < n_det)
        def _():
            pl.semaphore_signal(barrier, inc=1, device_id={"det": lax.rem(det + away, n_det)}, device_id_type=MESH)

    other_core = {"beam": beam + 1 - 2 * core}
    pl.semaphore_signal(barrier, inc=1, device_id=other_core, device_id_type=MESH)
    for away in (-1, 1):

        @pl.when(has[away])
        def _():
            for c in range(cores):
                pl.semaphore_signal(barrier, inc=1, device_id=chip_at(away, c), device_id_type=MESH)

    def tell(turn):
        for away in (-1, 1):

            @pl.when(has[away])
            def _():
                pl.semaphore_signal(relays.at[turn], inc=1, device_id=chip_at(away, core), device_id_type=MESH)

    def hear(turn):
        pl.semaphore_wait(relays.at[turn], beside)

    def remote(src, dst, send, recv, device):
        return pltpu.make_async_remote_copy(
            src_ref=src, dst_ref=dst, send_sem=send, recv_sem=recv, device_id=device, device_id_type=MESH
        )

    def depth_copy(away):
        return remote(ra_send, ra_recv.at[away], ra_ss.at[away], ra_rs.at[away], {"det": lax.rem(det - away + n_det, n_det)})

    def column_copy(away):
        return remote(rc_send, rc_recv.at[away], rc_ss.at[away], rc_rs.at[away], {"det": lax.rem(det + away, n_det)})

    def beam_copy(away):
        slot = n_beam - away
        return remote(ud_send, ud_recv.at[slot], ud_ss.at[away], ud_rs.at[slot], {"beam": beam_at(away)})

    def line_copy(part, away):
        slot = (n_beam - away) % n_beam
        if part == 1:
            src, rows, target = x_buf.at[0, :, pl.ds(nz, nz), :], pl.ds(nz, nz), slab
        elif part == 0:
            src, rows, target = x_buf.at[0, :, pl.ds(2 * nz - REACH, REACH), :], pl.ds(nz - REACH, REACH), slab_at(1)
        else:
            src, rows, target = x_buf.at[0, :, pl.ds(nz, REACH), :], pl.ds(2 * nz, REACH), slab_at(n_slab - 1)
        return remote(
            src, x_buf.at[slot, :, rows, :], x_ss.at[part, away], x_rs.at[part, slot], {"beam": beam_at(away), "slab": target}
        )

    order = sorted(range(n_beam), key=lambda away: abs(2 * away - n_beam))
    lines = [(part, away) for away in order for part in (0, 2)] + [(1, away) for away in order if away]

    def slab_copy(away, receiving):
        source = slab_at(away) if receiving else slab
        rows = pl.ds(pl.multiple_of(source * nz, nz), nz)
        slot = away if receiving else n_slab - away
        return remote(
            xl.at[:, pl.ds(nz, nz), :], la.at[:, rows, :], la_ss.at[away], la_rs.at[slot], {"slab": slab_at(away)}
        )

    for copy in small:
        copy.wait()
    sigma = [[cross[s, index[e]] * c1 for e in range(n_e)] for s in range(n_s)]
    lam_near = [lam[s] * c2 for s in range(n_s)]
    lam_before = [lam[s] * (c2 / c1) for s in range(n_s)]

    tile = BLOCK * nz

    def totals_of(value, block, dst):
        pair = split_pair(value.reshape(tile, ny))
        hl[block * tile : (block + 1) * tile] = pair
        dst[block : block + 1, :] = row_totals(pair)

    for chunk in range(CHUNKS):
        for z in range(nz):
            load(chunk, z).wait()
        for block in range(chunk * per_chunk, (chunk + 1) * per_chunk):
            rows = pl.ds(block * BLOCK, BLOCK)
            absorb = lam_near[0] * c_buf[0, rows]
            for s in range(1, n_s):
                absorb = absorb + lam_near[s] * c_buf[s, rows]
            totals_of(absorb, block, ra_send)
    pl.semaphore_wait(barrier, det + 1 + cores * beside)
    for away in range(1, n_det):

        @pl.when(det - away >= 0)
        def _():
            depth_copy(away).start()

    tell(0)

    def first(block, depth):
        depth = list(depth)
        for part in range(BLOCK // 4):
            rows = pl.ds(block * BLOCK + part * 4, 4)
            c = [c_buf[s, rows] for s in range(n_s)]
            for e in range(n_e):
                value = sigma[0][e] * c[0]
                for s in range(1, n_s):
                    value = value + sigma[s][e] * c[s]
                em[e, rows] = value
                for x in range(4):
                    inc[e, block * BLOCK + part * 4 + x] = jnp.exp(depth[e])
                    depth[e] = depth[e] - value[x]
        return tuple(depth)

    depth = lax.fori_loop(0, blocks, first, (jnp.zeros((nz, ny), F32),) * n_e)
    for e in range(n_e):
        ud_send[e] = depth[e]
    for away in range(1, n_beam):
        beam_copy(away).start()
    hear(0)
    tell(1)

    for away in range(1, n_det):

        @pl.when(det + away >= n_det)
        def _():
            ra_recv[away] = jnp.zeros_like(ra_send)

        @pl.when(det - away < 0)
        def _():
            rc_recv[away] = jnp.zeros_like(rc_send)

    no_halo = jnp.zeros((n_beam, n_e, REACH, ny), F32)

    @pl.when(slab == 0)
    def _():
        x_buf[:, :, nz - REACH : nz] = no_halo

    @pl.when(slab == n_slab - 1)
    def _():
        x_buf[:, :, 2 * nz : 2 * nz + REACH] = no_halo

    deep = lax.broadcasted_iota(jnp.int32, (2 * ny, ny), 0) % ny
    wide = lax.broadcasted_iota(jnp.int32, (2 * ny, ny), 1)
    beyond = jnp.where(deep > wide, -1.0, 0.0).astype(BF16)
    nearer_side = jnp.where(deep < wide, 1.0, 0.0).astype(BF16)

    for block in range(blocks):
        path = jnp.dot(hl[block * tile : (block + 1) * tile], beyond, preferred_element_type=F32)
        escape = jnp.exp(path).reshape(BLOCK, nz, ny)
        rows = pl.ds(block * BLOCK, BLOCK)
        for e in range(n_e):
            light = inc[e, rows] * escape
            inc[e, rows] = light
            em[e, rows] = em[e, rows] * light

    slices = lax.broadcasted_iota(jnp.int32, wt.shape, 0) - nz
    full = jnp.zeros(wt.shape, F32)
    for j in range(fan):
        tap = weight[j : j + 1, :].astype(F32)
        full = full + jnp.where(offset[...] + j == slices, tap, 0.0)
    wt[...] = full
    wx[...] = wt[pl.ds(pl.multiple_of(slab * nz, nz), 3 * nz), :]
    whole = wt[nz : nz + n_slab * nz, :]
    padded = jnp.concatenate([whole, jnp.zeros((128 - n_slab * nz, n_k), F32)], axis=0)
    wk[...] = jnp.transpose(padded)
    own = wx[nz : 2 * nz, :]
    for shift in range(2 * REACH + 1):
        other = wx[nz - REACH + shift : 2 * nz - REACH + shift, :]
        band[shift] = jnp.broadcast_to(jnp.sum(own * other, axis=1, keepdims=True), (nz, ny))
    load_measured.wait()
    for e in range(n_e):
        wm[e] = jnp.dot(own, meas[e], precision=HIGHEST, preferred_element_type=F32)

    hear(1)
    tell(2)
    hear(2)
    tell(3)
    for away in range(1, n_beam):
        beam_copy(away).wait_recv()
    upstream = jnp.zeros((n_e, nz, ny), F32)
    for slot in range(1, n_beam):
        upstream = upstream + jnp.where(beam + slot >= n_beam, 1.0, 0.0) * ud_recv[slot]
    up_buf[...] = jnp.exp(upstream)

    for away in range(1, n_det):

        @pl.when(det + away < n_det)
        def _():
            depth_copy(away).wait_recv()

    downstream = ra_recv[1]
    for away in range(2, n_det):
        downstream = downstream + ra_recv[away]
    for r, piece in enumerate(spread(jnp.exp(-downstream))):
        dmp[r * BLOCK : (r + 1) * BLOCK] = piece.reshape(BLOCK, nz, ny)

    def third(block, sums):
        rows = pl.ds(block * BLOCK, BLOCK)
        damp = dmp[rows]
        return tuple(sums[e] + jnp.sum(em[e, rows] * damp, axis=0) for e in range(n_e))

    sums = lax.fori_loop(0, blocks, third, (jnp.zeros((nz, ny), F32),) * n_e)
    for e in range(n_e):
        x_buf[0, e, nz : 2 * nz] = sums[e] * up_buf[e]
    send_if = {0: slab < n_slab - 1, 1: slab >= 0, 2: slab > 0}
    take_if = {0: slab > 0, 1: slab >= 0, 2: slab < n_slab - 1}
    for part, away in lines:

        @pl.when(send_if[part])
        def _():
            line_copy(part, away).start()

    hear(3)
    tell(4)

    def fourth(count, after):
        block = blocks - 1 - count
        after = list(after)
        for x in range(BLOCK - 1, -1, -1):
            row = block * BLOCK + x
            damp = dmp[row]
            for e in range(n_e):
                fluor = em[e, row] * damp
                inc[e, row] = inc[e, row] * damp - after[e]
                em[e, row] = fluor
                after[e] = after[e] + fluor
        return tuple(after)

    lax.fori_loop(0, blocks, fourth, (jnp.zeros((nz, ny), F32),) * n_e)

    def take_lines(wanted):
        for part, away in lines:
            if part in wanted:

                @pl.when(take_if[part])
                def _():
                    line_copy(part, away).wait_recv()

    def gather_lines(rows):
        total = x_buf[0, :, rows]
        for slot in range(1, n_beam):
            total = total + x_buf[slot, :, rows]
        xl[:, rows] = total
        return total

    take_lines((1,))
    own_lines = gather_lines(slice(nz, 2 * nz))
    hear(4)
    for away in range(1, n_slab):
        slab_copy(away, False).start()
    la[:, pl.ds(pl.multiple_of(slab * nz, nz), nz), :] = own_lines
    take_lines((0, 2))
    gather_lines(slice(nz - REACH, nz))
    gather_lines(slice(2 * nz, 2 * nz + REACH))
    further = jnp.zeros((n_e, nz, ny), F32)
    for slot in range(1, n_beam):
        further = further + jnp.where(beam + slot < n_beam, 1.0, 0.0) * x_buf[slot, :, nz : 2 * nz]
    back = []
    for e in range(n_e):
        value = band[0] * xl[e, nz - REACH : 2 * nz - REACH]
        for shift in range(1, 2 * REACH + 1):
            value = value + band[shift] * xl[e, nz - REACH + shift : 2 * nz - REACH + shift]
        back.append(value * (1.0 / 1.5) - wm[e])
    lit = [back[e] * up_buf[e] for e in range(n_e)]

    for block in range(blocks):
        rows = pl.ds(block * BLOCK, BLOCK)
        heavy = lit[0] * em[0, rows]
        for e in range(1, n_e):
            heavy = heavy + lit[e] * em[e, rows]
        totals_of(heavy, block, rc_send)
    for away in range(1, n_det):

        @pl.when(det + away < n_det)
        def _():
            column_copy(away).start()

    shade = [back[e] * further[e] for e in range(n_e)]
    mix, less = [], []
    for s in range(n_s):
        pull = [cross[s, index[e]] for e in range(n_e)]
        mix.append([pull[e] * lit[e] for e in range(n_e)])
        value = pull[0] * shade[0]
        for e in range(1, n_e):
            value = value + pull[e] * shade[e]
        less.append(value)

    for block in range(blocks):
        before = jnp.dot(hl[block * tile : (block + 1) * tile], nearer_side, preferred_element_type=F32)
        dmp[block * BLOCK : (block + 1) * BLOCK] = before.reshape(BLOCK, nz, ny)

    def sixth(block, carry):
        for part in range(BLOCK // 4):
            rows = pl.ds(block * BLOCK + part * 4, 4)
            term = [inc[e, rows] for e in range(n_e)]
            for s in range(n_s):
                value = mix[s][0] * term[0]
                for e in range(1, n_e):
                    value = value + mix[s][e] * term[e]
                part_out[s, rows] = value - less[s] - lam_before[s] * dmp[rows]
        return carry

    lax.fori_loop(0, blocks, sixth, 0)

    def take_columns():
        for away in range(1, n_det):

            @pl.when(det - away >= 0)
            def _():
                remote(rc_send, rc_recv.at[away], rc_ss.at[away], rc_rs.at[away], {"det": lax.rem(det + away, n_det)}).wait_recv()

    take_columns()
    for away in range(1, n_slab):
        slab_copy(away, True).wait_recv()
    share = n_k // (n_beam * n_slab)
    mine = pl.ds(pl.multiple_of((beam * n_slab + slab) * share, share), share)
    for e in range(n_e):
        signal = jnp.dot(wk[mine, 0 : n_slab * nz], la[e], precision=HIGHEST, preferred_element_type=F32)
        resid[e] = signal * (1.0 / 1.5) - meas[e, mine]

    nearer = rc_recv[1]
    for away in range(2, n_det):
        nearer = nearer + rc_recv[away]
    near_out[...] = nearer
    for s in range(n_s):
        lam_out[s] = jnp.full((nz, ny), lam_before[s], F32)

    for away in range(1, n_det):

        @pl.when(det - away >= 0)
        def _():
            depth_copy(away).wait_send()

        @pl.when(det + away < n_det)
        def _():
            column_copy(away).wait_send()

    for away in range(1, n_beam):
        beam_copy(away).wait_send()
    for part, away in lines:

        @pl.when(send_if[part])
        def _():
            line_copy(part, away).wait_send()

    for away in range(1, n_slab):
        slab_copy(away, False).wait_send()


def finish(part, near, lam_before, resid_in, out, resid, buf, out_sem):
    n_s, nx, nz, ny = part.shape
    step = nx // STORES
    resid[...] = resid_in[...]
    pieces = spread(near[...])

    def store(chunk, z):
        rows = pl.ds(chunk * step, step)
        return pltpu.make_async_copy(buf.at[:, rows, z, :], out.at[:, z, rows, :], out_sem.at[chunk, z])

    for chunk in range(STORES):
        for block in range(chunk * step // BLOCK, (chunk + 1) * step // BLOCK):
            rows = slice(block * BLOCK, (block + 1) * BLOCK)
            shift = pieces[block].reshape(BLOCK, nz, ny)
            for s in range(n_s):
                buf[s, rows] = part[s, rows] - lam_before[s] * shift
        for z in range(nz):
            store(chunk, z).start()
    for chunk in range(STORES):
        for z in range(nz):
            store(chunk, z).wait()


def solution(mesh):
    sizes = (mesh.shape["beam"], mesh.shape["det"], mesh.shape["slab"])
    n_beam, n_det, n_slab = sizes

    def shards(concentration, cross_section, line_attenuation, energy_index, fan_offset, fan_weight, measured):
        n_s, nz, nx, ny = concentration.shape
        n_e, n_k = measured.shape[0], measured.shape[1]
        share = n_k // (n_beam * n_slab)
        volume = pltpu.VMEM((n_e, nx, nz, ny), F32)
        compact = (nx * nz // 128, 128)
        dma = pltpu.SemaphoreType.DMA
        scratch = [
            pltpu.SMEM(cross_section.shape, F32),
            pltpu.SMEM(line_attenuation.shape, F32),
            pltpu.SMEM(energy_index.shape, jnp.int32),
            pltpu.VMEM((1, n_k), jnp.int32),
            pltpu.VMEM((fan_weight.shape[1], n_k), jnp.int32),
            pltpu.VMEM((n_s, nx, nz, ny), F32),
            volume,
            volume,
            pltpu.VMEM((nx, nz, ny), F32),
            pltpu.VMEM((nx * nz, 2 * ny), BF16),
            pltpu.VMEM((n_e, n_k, ny), F32),
            pltpu.VMEM(((n_slab + 2) * nz, n_k), F32),
            pltpu.VMEM((3 * nz, n_k), F32),
            pltpu.VMEM((n_k, 128), F32),
            pltpu.VMEM((2 * REACH + 1, nz, ny), F32),
            pltpu.VMEM((n_e, nz, ny), F32),
            pltpu.VMEM((n_e, nz, ny), F32),
            pltpu.VMEM(compact, F32),
            pltpu.VMEM((n_det, *compact), F32),
            pltpu.VMEM((n_e, nz, ny), F32),
            pltpu.VMEM((n_beam, n_e, nz, ny), F32),
            pltpu.VMEM((n_beam, n_e, 3 * nz, ny), F32),
            pltpu.VMEM((n_e, 3 * nz, ny), F32),
            pltpu.VMEM((n_e, n_slab * nz, ny), F32),
            pltpu.VMEM(compact, F32),
            pltpu.VMEM((n_det, *compact), F32),
            dma((STORES, nz)),
            dma((5,)),
            dma,
            dma((n_det,)),
            dma((n_det,)),
            dma((n_beam,)),
            dma((n_beam,)),
            dma((3, n_beam)),
            dma((3, n_beam)),
            dma((n_slab,)),
            dma((n_slab,)),
            dma((n_det,)),
            dma((n_det,)),
            pltpu.SemaphoreType.REGULAR((5,)),
        ]
        hbm = pl.BlockSpec(memory_space=pltpu.HBM)
        vmem = pl.BlockSpec(memory_space=pltpu.VMEM)
        share_shape = (n_e, share, ny)
        passed = pl.pallas_call(
            functools.partial(kernel, sizes),
            out_shape=(
                pltpu.VMEM((n_s, nx, nz, ny), F32),
                pltpu.VMEM(compact, F32),
                pltpu.VMEM((n_s, nz, ny), F32),
                pltpu.VMEM(share_shape, F32),
            ),
            in_specs=[hbm] * 7,
            out_specs=(vmem,) * 4,
            scratch_shapes=scratch,
            compiler_params=pltpu.CompilerParams(
                collective_id=0, has_side_effects=True, vmem_limit_bytes=28 * 2**20
            ),
        )(
            *(
                pltpu.with_memory_space_constraint(array, pltpu.HBM)
                for array in (
                    concentration,
                    cross_section,
                    line_attenuation,
                    energy_index,
                    fan_offset.reshape(1, n_k),
                    fan_weight.T,
                    measured,
                )
            )
        )
        return pl.pallas_call(
            finish,
            out_shape=(
                jax.ShapeDtypeStruct(concentration.shape, F32),
                jax.ShapeDtypeStruct(share_shape, F32),
            ),
            in_specs=[vmem] * 4,
            out_specs=(hbm, vmem),
            scratch_shapes=[pltpu.VMEM((n_s, nx, nz, ny), F32), dma((STORES, nz))],
            compiler_params=pltpu.CompilerParams(vmem_limit_bytes=16 * 2**20),
        )(*passed)

    in_specs = (P(None, "slab", "beam", "det"), P(), P(), P(), P(), P(), P(None, None, "det"))
    out_specs = (P(None, "slab", "beam", "det"), P(None, ("beam", "slab"), "det"))
    return jax.shard_map(shards, mesh=mesh, in_specs=in_specs, out_specs=out_specs, check_vma=False)
```

```python
import functools

import jax
import jax.numpy as jnp
from jax import lax
from jax.experimental import pallas as pl
from jax.experimental.pallas import tpu as pltpu
from jax.sharding import PartitionSpec as P

MESH = pl.DeviceIdType.MESH
F32 = jnp.float32
BF16 = jnp.bfloat16
HIGHEST = lax.Precision.HIGHEST
CHUNKS = 2
STORES = 4
BLOCK = 16
REACH = 3


def split_pair(value):
    high = value.astype(BF16)
    low = (value - high.astype(F32)).astype(BF16)
    return jnp.concatenate([high, low], axis=1)


def row_totals(pair):
    ones = jnp.ones((8, pair.shape[1]), BF16)
    total = lax.dot_general(ones, pair, (((1,), (1,)), ((), ())), preferred_element_type=F32)
    return total[0:1]


def spread(compact):
    rows = compact.shape[0]
    padded = jnp.concatenate([compact, jnp.zeros((128 - rows, 128), F32)], axis=0)
    turned = jnp.transpose(padded)
    return [jnp.broadcast_to(turned[:, r : r + 1], (128, 128)) for r in range(rows)]


def kernel(
    sizes, conc, cross_in, lam_in, index_in, offset_in, weight_in, measured, part_out, near_out, lam_out, la_out, wk_out, meas_out,
    cross, lam, index, offset, weight, c_buf, em, inc, dmp, hl, meas, wt, wx, wk, band, wm, up_buf,
    ra_send, ra_recv, ud_send, ud_recv, x_buf, xl, la, rc_send, rc_recv,
    in_sem, small_sem, meas_sem, ra_ss, ra_rs, ud_ss, ud_rs, x_ss, x_rs, la_ss, la_rs, rc_ss, rc_rs, relays,
):
    n_beam, n_det, n_slab = sizes
    n_s, nz, nx, ny = conc.shape
    n_e = measured.shape[0]
    n_k = measured.shape[1]
    fan = weight_in.shape[0]
    c1 = 1.5 / (nx * n_beam)
    c2 = 1.5 / (ny * n_det)
    blocks = nx // BLOCK
    step = nx // CHUNKS
    per_chunk = blocks // CHUNKS
    beam, det, slab = lax.axis_index("beam"), lax.axis_index("det"), lax.axis_index("slab")

    def load(chunk, z):
        rows = pl.ds(chunk * step, step)
        return pltpu.make_async_copy(conc.at[:, z, rows, :], c_buf.at[:, rows, z, :], in_sem.at[chunk, z])

    pairs = ((cross_in, cross), (lam_in, lam), (index_in, index), (offset_in, offset), (weight_in, weight))
    small = [pltpu.make_async_copy(src, dst, small_sem.at[n]) for n, (src, dst) in enumerate(pairs)]
    for copy in small:
        copy.start()
    for chunk in range(CHUNKS):
        for z in range(nz):
            load(chunk, z).start()
    load_measured = pltpu.make_async_copy(measured, meas, meas_sem)
    load_measured.start()

    def beam_at(away):
        return lax.rem(beam + away, n_beam)

    def slab_at(away):
        return lax.rem(slab + away, n_slab)

    cores = 2
    deep_chips = n_beam // cores
    chips = deep_chips * n_slab
    chip, core = slab * deep_chips + beam // cores, lax.rem(beam, cores)

    def chip_at(away, core_at):
        there = lax.rem(chip + away + chips, chips)
        return {"beam": lax.rem(there, deep_chips) * cores + core_at, "slab": there // deep_chips}

    has = {-1: chip > 0, 1: chip < chips - 1}
    beside = jnp.where(has[-1], 1, 0) + jnp.where(has[1], 1, 0)
    barrier = pltpu.get_barrier_semaphore()
    for away in range(1, n_det):

        @pl.when(det + away < n_det)
        def _():
            pl.semaphore_signal(barrier, inc=1, device_id={"det": lax.rem(det + away, n_det)}, device_id_type=MESH)

    other_core = {"beam": beam + 1 - 2 * core}
    pl.semaphore_signal(barrier, inc=1, device_id=other_core, device_id_type=MESH)
    for away in (-1, 1):

        @pl.when(has[away])
        def _():
            for c in range(cores):
                pl.semaphore_signal(barrier, inc=1, device_id=chip_at(away, c), device_id_type=MESH)

    def tell(turn):
        for away in (-1, 1):

            @pl.when(has[away])
            def _():
                pl.semaphore_signal(relays.at[turn], inc=1, device_id=chip_at(away, core), device_id_type=MESH)

    def hear(turn):
        pl.semaphore_wait(relays.at[turn], beside)

    def remote(src, dst, send, recv, device):
        return pltpu.make_async_remote_copy(
            src_ref=src, dst_ref=dst, send_sem=send, recv_sem=recv, device_id=device, device_id_type=MESH
        )

    def depth_copy(away):
        return remote(ra_send, ra_recv.at[away], ra_ss.at[away], ra_rs.at[away], {"det": lax.rem(det - away + n_det, n_det)})

    def column_copy(away):
        return remote(rc_send, rc_recv.at[away], rc_ss.at[away], rc_rs.at[away], {"det": lax.rem(det + away, n_det)})

    def beam_copy(away):
        slot = n_beam - away
        return remote(ud_send, ud_recv.at[slot], ud_ss.at[away], ud_rs.at[slot], {"beam": beam_at(away)})

    def line_copy(part, away):
        slot = (n_beam - away) % n_beam
        if part == 1:
            src, rows, target = x_buf.at[0, :, pl.ds(nz, nz), :], pl.ds(nz, nz), slab
        elif part == 0:
            src, rows, target = x_buf.at[0, :, pl.ds(2 * nz - REACH, REACH), :], pl.ds(nz - REACH, REACH), slab_at(1)
        else:
            src, rows, target = x_buf.at[0, :, pl.ds(nz, REACH), :], pl.ds(2 * nz, REACH), slab_at(n_slab - 1)
        return remote(
            src, x_buf.at[slot, :, rows, :], x_ss.at[part, away], x_rs.at[part, slot], {"beam": beam_at(away), "slab": target}
        )

    order = sorted(range(n_beam), key=lambda away: abs(2 * away - n_beam))
    lines = [(part, away) for away in order for part in (0, 2)] + [(1, away) for away in order if away]

    def slab_copy(away, receiving):
        source = slab_at(away) if receiving else slab
        rows = pl.ds(pl.multiple_of(source * nz, nz), nz)
        slot = away if receiving else n_slab - away
        return remote(
            xl.at[:, pl.ds(nz, nz), :], la.at[:, rows, :], la_ss.at[away], la_rs.at[slot], {"slab": slab_at(away)}
        )

    for copy in small:
        copy.wait()
    sigma = [[cross[s, index[e]] * c1 for e in range(n_e)] for s in range(n_s)]
    lam_near = [lam[s] * c2 for s in range(n_s)]
    lam_before = [lam[s] * (c2 / c1) for s in range(n_s)]

    tile = BLOCK * nz

    def totals_of(value, block, dst):
        pair = split_pair(value.reshape(tile, ny))
        hl[block * tile : (block + 1) * tile] = pair
        dst[block : block + 1, :] = row_totals(pair)

    for chunk in range(CHUNKS):
        for z in range(nz):
            load(chunk, z).wait()
        for block in range(chunk * per_chunk, (chunk + 1) * per_chunk):
            rows = pl.ds(block * BLOCK, BLOCK)
            absorb = lam_near[0] * c_buf[0, rows]
            for s in range(1, n_s):
                absorb = absorb + lam_near[s] * c_buf[s, rows]
            totals_of(absorb, block, ra_send)
    pl.semaphore_wait(barrier, det + 1 + cores * beside)
    for away in range(1, n_det):

        @pl.when(det - away >= 0)
        def _():
            depth_copy(away).start()

    tell(0)

    def first(block, depth):
        depth = list(depth)
        for part in range(BLOCK // 4):
            rows = pl.ds(block * BLOCK + part * 4, 4)
            c = [c_buf[s, rows] for s in range(n_s)]
            for e in range(n_e):
                value = sigma[0][e] * c[0]
                for s in range(1, n_s):
                    value = value + sigma[s][e] * c[s]
                em[e, rows] = value
                for x in range(4):
                    inc[e, block * BLOCK + part * 4 + x] = jnp.exp(depth[e])
                    depth[e] = depth[e] - value[x]
        return tuple(depth)

    depth = lax.fori_loop(0, blocks, first, (jnp.zeros((nz, ny), F32),) * n_e)
    for e in range(n_e):
        ud_send[e] = depth[e]
    for away in range(1, n_beam):
        beam_copy(away).start()
    hear(0)
    tell(1)

    for away in range(1, n_det):

        @pl.when(det + away >= n_det)
        def _():
            ra_recv[away] = jnp.zeros_like(ra_send)

        @pl.when(det - away < 0)
        def _():
            rc_recv[away] = jnp.zeros_like(rc_send)

    no_halo = jnp.zeros((n_beam, n_e, REACH, ny), F32)

    @pl.when(slab == 0)
    def _():
        x_buf[:, :, nz - REACH : nz] = no_halo

    @pl.when(slab == n_slab - 1)
    def _():
        x_buf[:, :, 2 * nz : 2 * nz + REACH] = no_halo

    deep = lax.broadcasted_iota(jnp.int32, (2 * ny, ny), 0) % ny
    wide = lax.broadcasted_iota(jnp.int32, (2 * ny, ny), 1)
    beyond = jnp.where(deep > wide, -1.0, 0.0).astype(BF16)
    nearer_side = jnp.where(deep < wide, 1.0, 0.0).astype(BF16)

    for block in range(blocks):
        path = jnp.dot(hl[block * tile : (block + 1) * tile], beyond, preferred_element_type=F32)
        escape = jnp.exp(path).reshape(BLOCK, nz, ny)
        rows = pl.ds(block * BLOCK, BLOCK)
        for e in range(n_e):
            light = inc[e, rows] * escape
            inc[e, rows] = light
            em[e, rows] = em[e, rows] * light

    slices = lax.broadcasted_iota(jnp.int32, wt.shape, 0) - nz
    full = jnp.zeros(wt.shape, F32)
    for j in range(fan):
        tap = weight[j : j + 1, :].astype(F32)
        full = full + jnp.where(offset[...] + j == slices, tap, 0.0)
    wt[...] = full
    wx[...] = wt[pl.ds(pl.multiple_of(slab * nz, nz), 3 * nz), :]
    whole = wt[nz : nz + n_slab * nz, :]
    padded = jnp.concatenate([whole, jnp.zeros((128 - n_slab * nz, n_k), F32)], axis=0)
    wk[...] = jnp.transpose(padded)
    own = wx[nz : 2 * nz, :]
    for shift in range(2 * REACH + 1):
        other = wx[nz - REACH + shift : 2 * nz - REACH + shift, :]
        band[shift] = jnp.broadcast_to(jnp.sum(own * other, axis=1, keepdims=True), (nz, ny))
    load_measured.wait()
    for e in range(n_e):
        wm[e] = jnp.dot(own, meas[e], precision=HIGHEST, preferred_element_type=F32)

    hear(1)
    tell(2)
    hear(2)
    tell(3)
    for away in range(1, n_beam):
        beam_copy(away).wait_recv()
    upstream = jnp.zeros((n_e, nz, ny), F32)
    for slot in range(1, n_beam):
        upstream = upstream + jnp.where(beam + slot >= n_beam, 1.0, 0.0) * ud_recv[slot]
    up_buf[...] = jnp.exp(upstream)

    for away in range(1, n_det):

        @pl.when(det + away < n_det)
        def _():
            depth_copy(away).wait_recv()

    downstream = ra_recv[1]
    for away in range(2, n_det):
        downstream = downstream + ra_recv[away]
    for r, piece in enumerate(spread(jnp.exp(-downstream))):
        dmp[r * BLOCK : (r + 1) * BLOCK] = piece.reshape(BLOCK, nz, ny)

    def third(block, sums):
        rows = pl.ds(block * BLOCK, BLOCK)
        damp = dmp[rows]
        return tuple(sums[e] + jnp.sum(em[e, rows] * damp, axis=0) for e in range(n_e))

    sums = lax.fori_loop(0, blocks, third, (jnp.zeros((nz, ny), F32),) * n_e)
    for e in range(n_e):
        x_buf[0, e, nz : 2 * nz] = sums[e] * up_buf[e]
    send_if = {0: slab < n_slab - 1, 1: slab >= 0, 2: slab > 0}
    take_if = {0: slab > 0, 1: slab >= 0, 2: slab < n_slab - 1}
    for part, away in lines:

        @pl.when(send_if[part])
        def _():
            line_copy(part, away).start()

    hear(3)
    tell(4)

    def fourth(count, after):
        block = blocks - 1 - count
        after = list(after)
        for x in range(BLOCK - 1, -1, -1):
            row = block * BLOCK + x
            damp = dmp[row]
            for e in range(n_e):
                fluor = em[e, row] * damp
                inc[e, row] = inc[e, row] * damp - after[e]
                em[e, row] = fluor
                after[e] = after[e] + fluor
        return tuple(after)

    lax.fori_loop(0, blocks, fourth, (jnp.zeros((nz, ny), F32),) * n_e)

    def take_lines(wanted):
        for part, away in lines:
            if part in wanted:

                @pl.when(take_if[part])
                def _():
                    line_copy(part, away).wait_recv()

    def gather_lines(rows):
        total = x_buf[0, :, rows]
        for slot in range(1, n_beam):
            total = total + x_buf[slot, :, rows]
        xl[:, rows] = total
        return total

    take_lines((1,))
    own_lines = gather_lines(slice(nz, 2 * nz))
    hear(4)
    for away in range(1, n_slab):
        slab_copy(away, False).start()
    la[:, pl.ds(pl.multiple_of(slab * nz, nz), nz), :] = own_lines
    take_lines((0, 2))
    gather_lines(slice(nz - REACH, nz))
    gather_lines(slice(2 * nz, 2 * nz + REACH))
    further = jnp.zeros((n_e, nz, ny), F32)
    for slot in range(1, n_beam):
        further = further + jnp.where(beam + slot < n_beam, 1.0, 0.0) * x_buf[slot, :, nz : 2 * nz]
    back = []
    for e in range(n_e):
        value = band[0] * xl[e, nz - REACH : 2 * nz - REACH]
        for shift in range(1, 2 * REACH + 1):
            value = value + band[shift] * xl[e, nz - REACH + shift : 2 * nz - REACH + shift]
        back.append(value * (1.0 / 1.5) - wm[e])
    lit = [back[e] * up_buf[e] for e in range(n_e)]

    for block in range(blocks):
        rows = pl.ds(block * BLOCK, BLOCK)
        heavy = lit[0] * em[0, rows]
        for e in range(1, n_e):
            heavy = heavy + lit[e] * em[e, rows]
        totals_of(heavy, block, rc_send)
    for away in range(1, n_det):

        @pl.when(det + away < n_det)
        def _():
            column_copy(away).start()

    shade = [back[e] * further[e] for e in range(n_e)]
    mix, less = [], []
    for s in range(n_s):
        pull = [cross[s, index[e]] for e in range(n_e)]
        mix.append([pull[e] * lit[e] for e in range(n_e)])
        value = pull[0] * shade[0]
        for e in range(1, n_e):
            value = value + pull[e] * shade[e]
        less.append(value)

    for block in range(blocks):
        before = jnp.dot(hl[block * tile : (block + 1) * tile], nearer_side, preferred_element_type=F32)
        dmp[block * BLOCK : (block + 1) * BLOCK] = before.reshape(BLOCK, nz, ny)

    def sixth(block, carry):
        for part in range(BLOCK // 4):
            rows = pl.ds(block * BLOCK + part * 4, 4)
            term = [inc[e, rows] for e in range(n_e)]
            for s in range(n_s):
                value = mix[s][0] * term[0]
                for e in range(1, n_e):
                    value = value + mix[s][e] * term[e]
                part_out[s, rows] = value - less[s] - lam_before[s] * dmp[rows]
        return carry

    lax.fori_loop(0, blocks, sixth, 0)

    def take_columns():
        for away in range(1, n_det):

            @pl.when(det - away >= 0)
            def _():
                remote(rc_send, rc_recv.at[away], rc_ss.at[away], rc_rs.at[away], {"det": lax.rem(det + away, n_det)}).wait_recv()

    share = n_k // (n_beam * n_slab)
    mine = pl.ds(pl.multiple_of((beam * n_slab + slab) * share, share), share)
    wk_out[...] = wk[mine]
    meas_out[...] = meas[:, mine]
    for s in range(n_s):
        lam_out[s] = jnp.full((nz, ny), lam_before[s], F32)
    for away in range(1, n_det):

        @pl.when(det - away >= 0)
        def _():
            depth_copy(away).wait_send()

    for away in range(1, n_beam):
        beam_copy(away).wait_send()
    for part, away in lines:

        @pl.when(send_if[part])
        def _():
            line_copy(part, away).wait_send()

    take_columns()
    for away in range(1, n_slab):
        slab_copy(away, True).wait_recv()
    la_out[...] = la[...]
    nearer = rc_recv[1]
    for away in range(2, n_det):
        nearer = nearer + rc_recv[away]
    near_out[...] = nearer

    for away in range(1, n_det):

        @pl.when(det + away < n_det)
        def _():
            column_copy(away).wait_send()

    for away in range(1, n_slab):
        slab_copy(away, False).wait_send()


def finish(part, near, lam_before, la, wk, meas, out, resid, buf, out_sem):
    n_s, nx, nz, ny = part.shape
    step = nx // STORES
    pieces = spread(near[...])

    def store(chunk, z):
        rows = pl.ds(chunk * step, step)
        return pltpu.make_async_copy(buf.at[:, rows, z, :], out.at[:, z, rows, :], out_sem.at[chunk, z])

    for chunk in range(STORES):
        for block in range(chunk * step // BLOCK, (chunk + 1) * step // BLOCK):
            rows = slice(block * BLOCK, (block + 1) * BLOCK)
            shift = pieces[block].reshape(BLOCK, nz, ny)
            for s in range(n_s):
                buf[s, rows] = part[s, rows] - lam_before[s] * shift
        for z in range(nz):
            store(chunk, z).start()
    for e in range(la.shape[0]):
        signal = jnp.dot(wk[:, 0 : la.shape[1]], la[e], precision=HIGHEST, preferred_element_type=F32)
        resid[e] = signal * (1.0 / 1.5) - meas[e]
    for chunk in range(STORES):
        for z in range(nz):
            store(chunk, z).wait()


def solution(mesh):
    sizes = (mesh.shape["beam"], mesh.shape["det"], mesh.shape["slab"])
    n_beam, n_det, n_slab = sizes

    def shards(concentration, cross_section, line_attenuation, energy_index, fan_offset, fan_weight, measured):
        n_s, nz, nx, ny = concentration.shape
        n_e, n_k = measured.shape[0], measured.shape[1]
        share = n_k // (n_beam * n_slab)
        volume = pltpu.VMEM((n_e, nx, nz, ny), F32)
        compact = (nx * nz // 128, 128)
        dma = pltpu.SemaphoreType.DMA
        scratch = [
            pltpu.SMEM(cross_section.shape, F32),
            pltpu.SMEM(line_attenuation.shape, F32),
            pltpu.SMEM(energy_index.shape, jnp.int32),
            pltpu.VMEM((1, n_k), jnp.int32),
            pltpu.VMEM((fan_weight.shape[1], n_k), jnp.int32),
            pltpu.VMEM((n_s, nx, nz, ny), F32),
            volume,
            volume,
            pltpu.VMEM((nx, nz, ny), F32),
            pltpu.VMEM((nx * nz, 2 * ny), BF16),
            pltpu.VMEM((n_e, n_k, ny), F32),
            pltpu.VMEM(((n_slab + 2) * nz, n_k), F32),
            pltpu.VMEM((3 * nz, n_k), F32),
            pltpu.VMEM((n_k, 128), F32),
            pltpu.VMEM((2 * REACH + 1, nz, ny), F32),
            pltpu.VMEM((n_e, nz, ny), F32),
            pltpu.VMEM((n_e, nz, ny), F32),
            pltpu.VMEM(compact, F32),
            pltpu.VMEM((n_det, *compact), F32),
            pltpu.VMEM((n_e, nz, ny), F32),
            pltpu.VMEM((n_beam, n_e, nz, ny), F32),
            pltpu.VMEM((n_beam, n_e, 3 * nz, ny), F32),
            pltpu.VMEM((n_e, 3 * nz, ny), F32),
            pltpu.VMEM((n_e, n_slab * nz, ny), F32),
            pltpu.VMEM(compact, F32),
            pltpu.VMEM((n_det, *compact), F32),
            dma((STORES, nz)),
            dma((5,)),
            dma,
            dma((n_det,)),
            dma((n_det,)),
            dma((n_beam,)),
            dma((n_beam,)),
            dma((3, n_beam)),
            dma((3, n_beam)),
            dma((n_slab,)),
            dma((n_slab,)),
            dma((n_det,)),
            dma((n_det,)),
            pltpu.SemaphoreType.REGULAR((5,)),
        ]
        hbm = pl.BlockSpec(memory_space=pltpu.HBM)
        vmem = pl.BlockSpec(memory_space=pltpu.VMEM)
        share_shape = (n_e, share, ny)
        passed = pl.pallas_call(
            functools.partial(kernel, sizes),
            out_shape=(
                pltpu.VMEM((n_s, nx, nz, ny), F32),
                pltpu.VMEM(compact, F32),
                pltpu.VMEM((n_s, nz, ny), F32),
                pltpu.VMEM((n_e, n_slab * nz, ny), F32),
                pltpu.VMEM((share, 128), F32),
                pltpu.VMEM(share_shape, F32),
            ),
            in_specs=[hbm] * 7,
            out_specs=(vmem,) * 6,
            scratch_shapes=scratch,
            compiler_params=pltpu.CompilerParams(
                collective_id=0, has_side_effects=True, vmem_limit_bytes=28 * 2**20
            ),
        )(
            *(
                pltpu.with_memory_space_constraint(array, pltpu.HBM)
                for array in (
                    concentration,
                    cross_section,
                    line_attenuation,
                    energy_index,
                    fan_offset.reshape(1, n_k),
                    fan_weight.T,
                    measured,
                )
            )
        )
        return pl.pallas_call(
            finish,
            out_shape=(
                jax.ShapeDtypeStruct(concentration.shape, F32),
                jax.ShapeDtypeStruct(share_shape, F32),
            ),
            in_specs=[vmem] * 6,
            out_specs=(hbm, vmem),
            scratch_shapes=[pltpu.VMEM((n_s, nx, nz, ny), F32), dma((STORES, nz))],
            compiler_params=pltpu.CompilerParams(vmem_limit_bytes=16 * 2**20),
        )(*passed)

    in_specs = (P(None, "slab", "beam", "det"), P(), P(), P(), P(), P(), P(None, None, "det"))
    out_specs = (P(None, "slab", "beam", "det"), P(None, ("beam", "slab"), "det"))
    return jax.shard_map(shards, mesh=mesh, in_specs=in_specs, out_specs=out_specs, check_vma=False)
```

```python
import functools

import jax
import jax.numpy as jnp
from jax import lax
from jax.experimental import pallas as pl
from jax.experimental.pallas import tpu as pltpu
from jax.sharding import PartitionSpec as P

MESH = pl.DeviceIdType.MESH
F32 = jnp.float32
BF16 = jnp.bfloat16
HIGHEST = lax.Precision.HIGHEST
CHUNKS = 2
STORES = 4
BLOCK = 16
REACH = 3


def split_pair(value):
    high = value.astype(BF16)
    low = (value - high.astype(F32)).astype(BF16)
    return jnp.concatenate([high, low], axis=1)


def row_totals(pair):
    ones = jnp.ones((8, pair.shape[1]), BF16)
    total = lax.dot_general(ones, pair, (((1,), (1,)), ((), ())), preferred_element_type=F32)
    return total[0:1]


def spread(compact):
    rows = compact.shape[0]
    padded = jnp.concatenate([compact, jnp.zeros((128 - rows, 128), F32)], axis=0)
    turned = jnp.transpose(padded)
    return [jnp.broadcast_to(turned[:, r : r + 1], (128, 128)) for r in range(rows)]


def kernel(
    sizes, conc, cross_in, lam_in, index_in, offset_in, weight_in, measured, part_out, near_out, lam_out, la_out, wk_out, meas_out,
    cross, lam, index, offset, weight, c_buf, em, inc, dmp, hl, meas, wt, wx, wk, band, wm, up_buf,
    ra_send, ra_recv, ud_send, ud_recv, x_buf, xl, la, rc_send, rc_recv,
    in_sem, small_sem, meas_sem, ra_ss, ra_rs, ud_ss, ud_rs, x_ss, x_rs, la_ss, la_rs, rc_ss, rc_rs, relays,
):
    n_beam, n_det, n_slab = sizes
    n_s, nz, nx, ny = conc.shape
    n_e = measured.shape[0]
    n_k = measured.shape[1]
    fan = weight_in.shape[0]
    c1 = 1.5 / (nx * n_beam)
    c2 = 1.5 / (ny * n_det)
    blocks = nx // BLOCK
    step = nx // CHUNKS
    per_chunk = blocks // CHUNKS
    beam, det, slab = lax.axis_index("beam"), lax.axis_index("det"), lax.axis_index("slab")

    def load(chunk, z):
        rows = pl.ds(chunk * step, step)
        return pltpu.make_async_copy(conc.at[:, z, rows, :], c_buf.at[:, rows, z, :], in_sem.at[chunk, z])

    pairs = ((cross_in, cross), (lam_in, lam), (index_in, index), (offset_in, offset), (weight_in, weight))
    small = [pltpu.make_async_copy(src, dst, small_sem.at[n]) for n, (src, dst) in enumerate(pairs)]
    for copy in small:
        copy.start()
    for chunk in range(CHUNKS):
        for z in range(nz):
            load(chunk, z).start()
    load_measured = pltpu.make_async_copy(measured, meas, meas_sem)
    load_measured.start()

    def beam_at(away):
        return lax.rem(beam + away, n_beam)

    def slab_at(away):
        return lax.rem(slab + away, n_slab)

    cores = 2
    deep_chips = n_beam // cores
    chips = deep_chips * n_slab
    chip, core = slab * deep_chips + beam // cores, lax.rem(beam, cores)

    def chip_at(away, core_at):
        there = lax.rem(chip + away + chips, chips)
        return {"beam": lax.rem(there, deep_chips) * cores + core_at, "slab": there // deep_chips}

    has = {-1: chip > 0, 1: chip < chips - 1}
    beside = jnp.where(has[-1], 1, 0) + jnp.where(has[1], 1, 0)
    barrier = pltpu.get_barrier_semaphore()
    for away in range(1, n_det):

        @pl.when(det + away < n_det)
        def _():
            pl.semaphore_signal(barrier, inc=1, device_id={"det": lax.rem(det + away, n_det)}, device_id_type=MESH)

    other_core = {"beam": beam + 1 - 2 * core}
    pl.semaphore_signal(barrier, inc=1, device_id=other_core, device_id_type=MESH)
    for away in (-1, 1):

        @pl.when(has[away])
        def _():
            for c in range(cores):
                pl.semaphore_signal(barrier, inc=1, device_id=chip_at(away, c), device_id_type=MESH)

    def tell(turn):
        for away in (-1, 1):

            @pl.when(has[away])
            def _():
                pl.semaphore_signal(relays.at[turn], inc=1, device_id=chip_at(away, core), device_id_type=MESH)

    def hear(turn):
        pl.semaphore_wait(relays.at[turn], beside)

    def remote(src, dst, send, recv, device):
        return pltpu.make_async_remote_copy(
            src_ref=src, dst_ref=dst, send_sem=send, recv_sem=recv, device_id=device, device_id_type=MESH
        )

    def depth_copy(away):
        return remote(ra_send, ra_recv.at[away], ra_ss.at[away], ra_rs.at[away], {"det": lax.rem(det - away + n_det, n_det)})

    def column_copy(away):
        return remote(rc_send, rc_recv.at[away], rc_ss.at[away], rc_rs.at[away], {"det": lax.rem(det + away, n_det)})

    def beam_copy(away):
        slot = n_beam - away
        return remote(ud_send, ud_recv.at[slot], ud_ss.at[away], ud_rs.at[slot], {"beam": beam_at(away)})

    def line_copy(part, away):
        slot = (n_beam - away) % n_beam
        if part == 1:
            src, rows, target = x_buf.at[0, :, pl.ds(nz, nz), :], pl.ds(nz, nz), slab
        elif part == 0:
            src, rows, target = x_buf.at[0, :, pl.ds(2 * nz - REACH, REACH), :], pl.ds(nz - REACH, REACH), slab_at(1)
        else:
            src, rows, target = x_buf.at[0, :, pl.ds(nz, REACH), :], pl.ds(2 * nz, REACH), slab_at(n_slab - 1)
        return remote(
            src, x_buf.at[slot, :, rows, :], x_ss.at[part, away], x_rs.at[part, slot], {"beam": beam_at(away), "slab": target}
        )

    order = sorted(range(n_beam), key=lambda away: abs(2 * away - n_beam))
    halos = [(part, away) for away in order for part in (0, 2)]
    lines = halos[:2] + [(1, away) for away in order if away] + halos[2:]

    def slab_copy(away, receiving):
        source = slab_at(away) if receiving else slab
        rows = pl.ds(pl.multiple_of(source * nz, nz), nz)
        slot = away if receiving else n_slab - away
        return remote(
            xl.at[:, pl.ds(nz, nz), :], la.at[:, rows, :], la_ss.at[away], la_rs.at[slot], {"slab": slab_at(away)}
        )

    for copy in small:
        copy.wait()
    sigma = [[cross[s, index[e]] * c1 for e in range(n_e)] for s in range(n_s)]
    lam_near = [lam[s] * c2 for s in range(n_s)]
    lam_before = [lam[s] * (c2 / c1) for s in range(n_s)]

    tile = BLOCK * nz

    def totals_of(value, block, dst):
        pair = split_pair(value.reshape(tile, ny))
        hl[block * tile : (block + 1) * tile] = pair
        dst[block : block + 1, :] = row_totals(pair)

    for chunk in range(CHUNKS):
        for z in range(nz):
            load(chunk, z).wait()
        for block in range(chunk * per_chunk, (chunk + 1) * per_chunk):
            rows = pl.ds(block * BLOCK, BLOCK)
            absorb = lam_near[0] * c_buf[0, rows]
            for s in range(1, n_s):
                absorb = absorb + lam_near[s] * c_buf[s, rows]
            totals_of(absorb, block, ra_send)
    pl.semaphore_wait(barrier, det + 1 + cores * beside)
    for away in range(1, n_det):

        @pl.when(det - away >= 0)
        def _():
            depth_copy(away).start()

    tell(0)

    def first(block, depth):
        depth = list(depth)
        for part in range(BLOCK // 4):
            rows = pl.ds(block * BLOCK + part * 4, 4)
            c = [c_buf[s, rows] for s in range(n_s)]
            for e in range(n_e):
                value = sigma[0][e] * c[0]
                for s in range(1, n_s):
                    value = value + sigma[s][e] * c[s]
                em[e, rows] = value
                for x in range(4):
                    inc[e, block * BLOCK + part * 4 + x] = jnp.exp(depth[e])
                    depth[e] = depth[e] - value[x]
        return tuple(depth)

    depth = lax.fori_loop(0, blocks, first, (jnp.zeros((nz, ny), F32),) * n_e)
    for e in range(n_e):
        ud_send[e] = depth[e]
    for away in range(1, n_beam):
        beam_copy(away).start()
    hear(0)
    tell(1)

    for away in range(1, n_det):

        @pl.when(det + away >= n_det)
        def _():
            ra_recv[away] = jnp.zeros_like(ra_send)

        @pl.when(det - away < 0)
        def _():
            rc_recv[away] = jnp.zeros_like(rc_send)

    no_halo = jnp.zeros((n_beam, n_e, REACH, ny), F32)

    @pl.when(slab == 0)
    def _():
        x_buf[:, :, nz - REACH : nz] = no_halo

    @pl.when(slab == n_slab - 1)
    def _():
        x_buf[:, :, 2 * nz : 2 * nz + REACH] = no_halo

    deep = lax.broadcasted_iota(jnp.int32, (2 * ny, ny), 0) % ny
    wide = lax.broadcasted_iota(jnp.int32, (2 * ny, ny), 1)
    beyond = jnp.where(deep > wide, -1.0, 0.0).astype(BF16)
    nearer_side = jnp.where(deep < wide, 1.0, 0.0).astype(BF16)

    for block in range(blocks):
        path = jnp.dot(hl[block * tile : (block + 1) * tile], beyond, preferred_element_type=F32)
        escape = jnp.exp(path).reshape(BLOCK, nz, ny)
        rows = pl.ds(block * BLOCK, BLOCK)
        for e in range(n_e):
            light = inc[e, rows] * escape
            inc[e, rows] = light
            em[e, rows] = em[e, rows] * light

    slices = lax.broadcasted_iota(jnp.int32, wt.shape, 0) - nz
    full = jnp.zeros(wt.shape, F32)
    for j in range(fan):
        tap = weight[j : j + 1, :].astype(F32)
        full = full + jnp.where(offset[...] + j == slices, tap, 0.0)
    wt[...] = full
    wx[...] = wt[pl.ds(pl.multiple_of(slab * nz, nz), 3 * nz), :]
    whole = wt[nz : nz + n_slab * nz, :]
    padded = jnp.concatenate([whole, jnp.zeros((128 - n_slab * nz, n_k), F32)], axis=0)
    wk[...] = jnp.transpose(padded)
    own = wx[nz : 2 * nz, :]
    for shift in range(2 * REACH + 1):
        other = wx[nz - REACH + shift : 2 * nz - REACH + shift, :]
        band[shift] = jnp.broadcast_to(jnp.sum(own * other, axis=1, keepdims=True), (nz, ny))
    load_measured.wait()
    for e in range(n_e):
        wm[e] = jnp.dot(own, meas[e], precision=HIGHEST, preferred_element_type=F32)

    hear(1)
    tell(2)
    hear(2)
    tell(3)
    for away in range(1, n_beam):
        beam_copy(away).wait_recv()
    upstream = jnp.zeros((n_e, nz, ny), F32)
    for slot in range(1, n_beam):
        upstream = upstream + jnp.where(beam + slot >= n_beam, 1.0, 0.0) * ud_recv[slot]
    up_buf[...] = jnp.exp(upstream)

    for away in range(1, n_det):

        @pl.when(det + away < n_det)
        def _():
            depth_copy(away).wait_recv()

    downstream = ra_recv[1]
    for away in range(2, n_det):
        downstream = downstream + ra_recv[away]
    for r, piece in enumerate(spread(jnp.exp(-downstream))):
        dmp[r * BLOCK : (r + 1) * BLOCK] = piece.reshape(BLOCK, nz, ny)

    def third(block, sums):
        rows = pl.ds(block * BLOCK, BLOCK)
        damp = dmp[rows]
        return tuple(sums[e] + jnp.sum(em[e, rows] * damp, axis=0) for e in range(n_e))

    sums = lax.fori_loop(0, blocks, third, (jnp.zeros((nz, ny), F32),) * n_e)
    for e in range(n_e):
        x_buf[0, e, nz : 2 * nz] = sums[e] * up_buf[e]
    send_if = {0: slab < n_slab - 1, 1: slab >= 0, 2: slab > 0}
    take_if = {0: slab > 0, 1: slab >= 0, 2: slab < n_slab - 1}
    for part, away in lines:

        @pl.when(send_if[part])
        def _():
            line_copy(part, away).start()

    hear(3)
    tell(4)

    def fourth(count, after):
        block = blocks - 1 - count
        after = list(after)
        for x in range(BLOCK - 1, -1, -1):
            row = block * BLOCK + x
            damp = dmp[row]
            for e in range(n_e):
                fluor = em[e, row] * damp
                inc[e, row] = inc[e, row] * damp - after[e]
                em[e, row] = fluor
                after[e] = after[e] + fluor
        return tuple(after)

    lax.fori_loop(0, blocks, fourth, (jnp.zeros((nz, ny), F32),) * n_e)

    def take_lines(wanted):
        for part, away in lines:
            if part in wanted:

                @pl.when(take_if[part])
                def _():
                    line_copy(part, away).wait_recv()

    def gather_lines(rows):
        total = x_buf[0, :, rows]
        for slot in range(1, n_beam):
            total = total + x_buf[slot, :, rows]
        xl[:, rows] = total
        return total

    take_lines((1,))
    own_lines = gather_lines(slice(nz, 2 * nz))
    hear(4)
    for away in range(1, n_slab):
        slab_copy(away, False).start()
    la[:, pl.ds(pl.multiple_of(slab * nz, nz), nz), :] = own_lines
    take_lines((0, 2))
    gather_lines(slice(nz - REACH, nz))
    gather_lines(slice(2 * nz, 2 * nz + REACH))
    further = jnp.zeros((n_e, nz, ny), F32)
    for slot in range(1, n_beam):
        further = further + jnp.where(beam + slot < n_beam, 1.0, 0.0) * x_buf[slot, :, nz : 2 * nz]
    back = []
    for e in range(n_e):
        value = band[0] * xl[e, nz - REACH : 2 * nz - REACH]
        for shift in range(1, 2 * REACH + 1):
            value = value + band[shift] * xl[e, nz - REACH + shift : 2 * nz - REACH + shift]
        back.append(value * (1.0 / 1.5) - wm[e])
    lit = [back[e] * up_buf[e] for e in range(n_e)]

    for block in range(blocks):
        rows = pl.ds(block * BLOCK, BLOCK)
        heavy = lit[0] * em[0, rows]
        for e in range(1, n_e):
            heavy = heavy + lit[e] * em[e, rows]
        totals_of(heavy, block, rc_send)
    for away in range(1, n_det):

        @pl.when(det + away < n_det)
        def _():
            column_copy(away).start()

    shade = [back[e] * further[e] for e in range(n_e)]
    mix, less = [], []
    for s in range(n_s):
        pull = [cross[s, index[e]] for e in range(n_e)]
        mix.append([pull[e] * lit[e] for e in range(n_e)])
        value = pull[0] * shade[0]
        for e in range(1, n_e):
            value = value + pull[e] * shade[e]
        less.append(value)

    for block in range(blocks):
        before = jnp.dot(hl[block * tile : (block + 1) * tile], nearer_side, preferred_element_type=F32)
        dmp[block * BLOCK : (block + 1) * BLOCK] = before.reshape(BLOCK, nz, ny)

    def sixth(block, carry):
        for part in range(BLOCK // 4):
            rows = pl.ds(block * BLOCK + part * 4, 4)
            term = [inc[e, rows] for e in range(n_e)]
            for s in range(n_s):
                value = mix[s][0] * term[0]
                for e in range(1, n_e):
                    value = value + mix[s][e] * term[e]
                part_out[s, rows] = value - less[s] - lam_before[s] * dmp[rows]
        return carry

    lax.fori_loop(0, blocks, sixth, 0)

    def take_columns():
        for away in range(1, n_det):

            @pl.when(det - away >= 0)
            def _():
                remote(rc_send, rc_recv.at[away], rc_ss.at[away], rc_rs.at[away], {"det": lax.rem(det + away, n_det)}).wait_recv()

    share = n_k // (n_beam * n_slab)
    mine = pl.ds(pl.multiple_of((beam * n_slab + slab) * share, share), share)
    wk_out[...] = wk[mine]
    meas_out[...] = meas[:, mine]
    for s in range(n_s):
        lam_out[s] = jnp.full((nz, ny), lam_before[s], F32)
    for away in range(1, n_det):

        @pl.when(det - away >= 0)
        def _():
            depth_copy(away).wait_send()

    for away in range(1, n_beam):
        beam_copy(away).wait_send()
    for part, away in lines:

        @pl.when(send_if[part])
        def _():
            line_copy(part, away).wait_send()

    take_columns()
    for away in range(1, n_slab):
        slab_copy(away, True).wait_recv()
    la_out[...] = la[...]
    nearer = rc_recv[1]
    for away in range(2, n_det):
        nearer = nearer + rc_recv[away]
    near_out[...] = nearer

    for away in range(1, n_det):

        @pl.when(det + away < n_det)
        def _():
            column_copy(away).wait_send()

    for away in range(1, n_slab):
        slab_copy(away, False).wait_send()


def finish(part, near, lam_before, la, wk, meas, out, resid, buf, out_sem):
    n_s, nx, nz, ny = part.shape
    step = nx // STORES
    pieces = spread(near[...])

    def store(chunk, z):
        rows = pl.ds(chunk * step, step)
        return pltpu.make_async_copy(buf.at[:, rows, z, :], out.at[:, z, rows, :], out_sem.at[chunk, z])

    for chunk in range(STORES):
        for block in range(chunk * step // BLOCK, (chunk + 1) * step // BLOCK):
            rows = slice(block * BLOCK, (block + 1) * BLOCK)
            shift = pieces[block].reshape(BLOCK, nz, ny)
            for s in range(n_s):
                buf[s, rows] = part[s, rows] - lam_before[s] * shift
        for z in range(nz):
            store(chunk, z).start()
    for e in range(la.shape[0]):
        signal = jnp.dot(wk[:, 0 : la.shape[1]], la[e], precision=HIGHEST, preferred_element_type=F32)
        resid[e] = signal * (1.0 / 1.5) - meas[e]
    for chunk in range(STORES):
        for z in range(nz):
            store(chunk, z).wait()


def solution(mesh):
    sizes = (mesh.shape["beam"], mesh.shape["det"], mesh.shape["slab"])
    n_beam, n_det, n_slab = sizes

    def shards(concentration, cross_section, line_attenuation, energy_index, fan_offset, fan_weight, measured):
        n_s, nz, nx, ny = concentration.shape
        n_e, n_k = measured.shape[0], measured.shape[1]
        share = n_k // (n_beam * n_slab)
        volume = pltpu.VMEM((n_e, nx, nz, ny), F32)
        compact = (nx * nz // 128, 128)
        dma = pltpu.SemaphoreType.DMA
        scratch = [
            pltpu.SMEM(cross_section.shape, F32),
            pltpu.SMEM(line_attenuation.shape, F32),
            pltpu.SMEM(energy_index.shape, jnp.int32),
            pltpu.VMEM((1, n_k), jnp.int32),
            pltpu.VMEM((fan_weight.shape[1], n_k), jnp.int32),
            pltpu.VMEM((n_s, nx, nz, ny), F32),
            volume,
            volume,
            pltpu.VMEM((nx, nz, ny), F32),
            pltpu.VMEM((nx * nz, 2 * ny), BF16),
            pltpu.VMEM((n_e, n_k, ny), F32),
            pltpu.VMEM(((n_slab + 2) * nz, n_k), F32),
            pltpu.VMEM((3 * nz, n_k), F32),
            pltpu.VMEM((n_k, 128), F32),
            pltpu.VMEM((2 * REACH + 1, nz, ny), F32),
            pltpu.VMEM((n_e, nz, ny), F32),
            pltpu.VMEM((n_e, nz, ny), F32),
            pltpu.VMEM(compact, F32),
            pltpu.VMEM((n_det, *compact), F32),
            pltpu.VMEM((n_e, nz, ny), F32),
            pltpu.VMEM((n_beam, n_e, nz, ny), F32),
            pltpu.VMEM((n_beam, n_e, 3 * nz, ny), F32),
            pltpu.VMEM((n_e, 3 * nz, ny), F32),
            pltpu.VMEM((n_e, n_slab * nz, ny), F32),
            pltpu.VMEM(compact, F32),
            pltpu.VMEM((n_det, *compact), F32),
            dma((STORES, nz)),
            dma((5,)),
            dma,
            dma((n_det,)),
            dma((n_det,)),
            dma((n_beam,)),
            dma((n_beam,)),
            dma((3, n_beam)),
            dma((3, n_beam)),
            dma((n_slab,)),
            dma((n_slab,)),
            dma((n_det,)),
            dma((n_det,)),
            pltpu.SemaphoreType.REGULAR((5,)),
        ]
        hbm = pl.BlockSpec(memory_space=pltpu.HBM)
        vmem = pl.BlockSpec(memory_space=pltpu.VMEM)
        share_shape = (n_e, share, ny)
        passed = pl.pallas_call(
            functools.partial(kernel, sizes),
            out_shape=(
                pltpu.VMEM((n_s, nx, nz, ny), F32),
                pltpu.VMEM(compact, F32),
                pltpu.VMEM((n_s, nz, ny), F32),
                pltpu.VMEM((n_e, n_slab * nz, ny), F32),
                pltpu.VMEM((share, 128), F32),
                pltpu.VMEM(share_shape, F32),
            ),
            in_specs=[hbm] * 7,
            out_specs=(vmem,) * 6,
            scratch_shapes=scratch,
            compiler_params=pltpu.CompilerParams(
                collective_id=0, has_side_effects=True, vmem_limit_bytes=28 * 2**20
            ),
        )(
            *(
                pltpu.with_memory_space_constraint(array, pltpu.HBM)
                for array in (
                    concentration,
                    cross_section,
                    line_attenuation,
                    energy_index,
                    fan_offset.reshape(1, n_k),
                    fan_weight.T,
                    measured,
                )
            )
        )
        return pl.pallas_call(
            finish,
            out_shape=(
                jax.ShapeDtypeStruct(concentration.shape, F32),
                jax.ShapeDtypeStruct(share_shape, F32),
            ),
            in_specs=[vmem] * 6,
            out_specs=(hbm, vmem),
            scratch_shapes=[pltpu.VMEM((n_s, nx, nz, ny), F32), dma((STORES, nz))],
            compiler_params=pltpu.CompilerParams(vmem_limit_bytes=16 * 2**20),
        )(*passed)

    in_specs = (P(None, "slab", "beam", "det"), P(), P(), P(), P(), P(), P(None, None, "det"))
    out_specs = (P(None, "slab", "beam", "det"), P(None, ("beam", "slab"), "det"))
    return jax.shard_map(shards, mesh=mesh, in_specs=in_specs, out_specs=out_specs, check_vma=False)
```
